256 devices in a mesh: smp: 8 (over x, core), proto: 32 (over z, y).
Axes of the slice: x: 4, y: 4, z: 8, core: 2. Of those that a mesh axis runs over, the one named last changes fastest.
Arguments:
- teacher_feats: float32 [4096, 384], P('smp'), may hold values from -11 to 11, as said below
- student_feats: float32 [4096, 384], P('smp'), may hold values from -15 to 15, as said below
- prototypes: float32 [384, 131072], P(None, 'proto'), may hold values from -0.25 to 0.25
Outputs:
- grad_feats: float32 [4096, 384], P('smp')
- grad_protos: float32 [384, 131072], P('smp', 'proto')
The draws below stay inside these ranges and needn't reach their ends.
Inputs may be any that keep to these rules, and one draw needn't show every extreme that they name: `teacher_feats`: values of the teacher features of one crop. `student_feats`: values of the student features of one crop.
All inputs are finite; a program needn't handle non-finite values.
Results may differ from the reference program's by a relative error of at most 0.0003.
Values sent between devices are 32-bit elements; how exact they have to be, the bound alone decides.
A program may use at most 128 MiB of HBM per device.

```python
import jax
import jax.numpy as jnp
from jax import lax

D = 384
PROTO_DEV = 4096
ITERS = 3
CROPS = 4096
PROTOS = 131072


def prototype_values(key):
    matrix = jax.random.normal(key, (D, PROTOS), jnp.float32) * D ** (-0.5)
    return jnp.clip(matrix, -0.25, 0.25)


def feature_values(key, spike_scale):
    scale_key, spike_key, value_key = jax.random.split(key, 3)
    row_scale = jnp.exp(jax.random.uniform(scale_key, (CROPS,), jnp.float32, jnp.log(0.06), jnp.log(0.6)))
    spiked = jax.random.randint(spike_key, (CROPS,), 0, 64) == 0
    row_scale = jnp.where(spiked & (spike_scale > 0.0), spike_scale, row_scale)
    values = jnp.clip(jax.random.normal(value_key, (CROPS, D), jnp.float32), -6.0, 6.0)
    return values * row_scale[:, None]


def aligned_values(key, values, matrix, low_strength, high_strength):
    key = jax.random.fold_in(key, 5)
    index_key, offset_key, strength_key = jax.random.split(key, 3)
    columns = jax.random.randint(index_key, (CROPS,), 0, PROTOS)
    picked = jnp.take(matrix, columns, axis=1).T
    offset = jax.random.randint(offset_key, (), 0, 8)
    aligned = (jnp.arange(CROPS) + offset) % 8 == 0
    strength = jax.random.uniform(strength_key, (CROPS,), jnp.float32, low_strength, high_strength)
    return jnp.where(aligned[:, None], picked * strength[:, None], values)


def draw_prototypes(key, part):
    return prototype_values(key)


def draw_teacher_feats(key, part):
    matrix = prototype_values(key)
    key = jax.random.fold_in(key, 11)
    return aligned_values(key, feature_values(key, 0.0), matrix, 14.0, 28.0)


def draw_student_feats(key, part):
    matrix = prototype_values(key)
    key = jax.random.fold_in(key, 23)
    return aligned_values(key, feature_values(key, 0.0), matrix, 20.0, 40.0)


def setup_inputs(seed: int = 0) -> dict:
    arg_keys = jax.random.split(jax.random.key(seed), 4)
    return {
        "teacher_feats": draw_teacher_feats(jax.random.fold_in(arg_keys[3], 71), 0),
        "student_feats": draw_student_feats(jax.random.fold_in(arg_keys[3], 71), 0),
        "prototypes": draw_prototypes(jax.random.fold_in(arg_keys[3], 71), 0),
    }


teacher_temp = 0.07
student_temp = 0.1
highest = lax.Precision.HIGHEST


def reference(teacher_feats, student_feats, prototypes):
    count = PROTOS // PROTO_DEV
    blocks = prototypes.reshape(D, count, PROTO_DEV).transpose(1, 0, 2)

    def teacher_block(weights):
        return jnp.dot(teacher_feats, weights, precision=highest, preferred_element_type=jnp.float32) / teacher_temp

    def student_block(weights):
        return jnp.dot(student_feats, weights, precision=highest, preferred_element_type=jnp.float32) / student_temp

    peaks = lax.map(lambda weights: jnp.max(teacher_block(weights), axis=0), blocks)
    crop_scale = jnp.ones((CROPS,), jnp.float32)
    proto_scale = jnp.ones((count, PROTO_DEV), jnp.float32)
    for step in range(ITERS):
        def sweep(carry, inputs):
            weights, peak = inputs
            expo = jnp.exp(teacher_block(weights) - peak[None, :])
            scale = 1.0 / jnp.dot(crop_scale, expo, precision=highest)
            return carry + jnp.dot(expo, scale, precision=highest), scale

        mass, proto_scale = lax.scan(sweep, jnp.zeros((CROPS,), jnp.float32), (blocks, peaks))
        crop_scale = 1.0 / mass

    def row_stats(carry, weights):
        top, total = carry
        scores = student_block(weights)
        new_top = jnp.maximum(top, jnp.max(scores, axis=1))
        total = total * jnp.exp(top - new_top) + jnp.sum(jnp.exp(scores - new_top[:, None]), axis=1)
        return (new_top, total), None

    start = (jnp.full((CROPS,), -jnp.inf, jnp.float32), jnp.zeros((CROPS,), jnp.float32))
    (row_top, row_total), unused = lax.scan(row_stats, start, blocks)

    def final(carry, inputs):
        weights, peak, scale = inputs
        expo = jnp.exp(teacher_block(weights) - peak[None, :])
        targets = crop_scale[:, None] * expo * scale[None, :]
        probs = jnp.exp(student_block(weights) - row_top[:, None]) / row_total[:, None]
        dlogits = probs - targets
        carry = carry + lax.dot_general(dlogits, weights, (((1,), (1,)), ((), ())), precision=highest, preferred_element_type=jnp.float32) / student_temp
        grad_block = lax.dot_general(student_feats, dlogits, (((0,), (0,)), ((), ())), precision=highest, preferred_element_type=jnp.float32) / student_temp
        return carry, grad_block

    grad_feats, grad_blocks = lax.scan(final, jnp.zeros((CROPS, D), jnp.float32), (blocks, peaks, proto_scale))
    grad_protos = grad_blocks.transpose(1, 0, 2).reshape(D, PROTOS)
    return grad_feats, grad_protos
```

```python
import functools

import jax
import jax.numpy as jnp
from jax import lax
from jax.experimental import pallas as pl
from jax.experimental.pallas import tpu as pltpu
from jax.sharding import PartitionSpec as P

ITERS = 3
TEACHER_TEMP = 0.07
STUDENT_TEMP = 0.1
LOG2E = 1.4426950408889634

YN = 4
TILE = 512
LANES = 128
MESH = pl.DeviceIdType.MESH
f32 = jnp.float32
bf16 = jnp.bfloat16


def mm(a, b):
    return jnp.dot(a, b, preferred_element_type=f32)


def mm_t(a, b):
    return lax.dot_general(a, b, (((1,), (1,)), ((), ())), preferred_element_type=f32)


def split(v):
    hi = v.astype(bf16)
    return hi, (v - hi.astype(f32)).astype(bf16)


def kernel(
    SN,
    PN,
    t_hbm,
    s_hbm,
    p_hbm,
    gf_out,
    gp_out,
    feats,
    thh,
    tl,
    shh,
    sl,
    st,
    phl,
    e,
    q,
    dh,
    dl,
    cola,
    cola_in,
    col,
    col_in,
    pscale,
    peakf,
    acc,
    mx,
    cb,
    ab,
    rowm,
    row_y,
    row_z,
    rowt,
    stat,
    stat_y,
    stat_t,
    stat_z,
    gfacc,
    gfs,
    gfy,
    gfz,
    gft,
    gfz2,
    cr,
    xa,
    xb,
    load_sem,
    cs_sem,
    cr_sem,
    rys_sem,
    ryr_sem,
    rzs_sem,
    rzr_sem,
    sts_sem,
    str_sem,
    gs_sem,
    gr_sem,
    ks_sem,
    kr_sem,
    xs_sem,
    xr_sem,
):
    ZN = PN // YN
    XN = SN // 2
    rows, width = t_hbm.shape
    tiles = p_hbm.shape[1] // TILE
    per = TILE // LANES
    blocks = rows // LANES
    s = lax.axis_index("smp")
    p = lax.axis_index("proto")
    x = s // 2
    c = s % 2
    z = p // YN
    y = p % YN
    sibling = (2 * x + 1 - c, p)
    right = (2 * ((x + 1) % XN) + c, p)
    left = (2 * ((x + XN - 1) % XN) + c, p)
    smp_peers = [((s + d) % SN, p) for d in range(1, SN)]
    y_peers = [(s, z * YN + (y + d) % YN) for d in range(1, YN)]
    z_peers = [(s, ((z + d) % ZN) * YN + y) for d in range(1, ZN)]

    def rc(src, dst, ss, rs, dev):
        return pltpu.make_async_remote_copy(
            src_ref=src, dst_ref=dst, send_sem=ss, recv_sem=rs, device_id=dev, device_id_type=MESH
        )

    barrier = pltpu.get_barrier_semaphore()
    for dev in smp_peers + y_peers + z_peers:
        pl.semaphore_signal(barrier, inc=1, device_id=dev, device_id_type=MESH)

    load_t = pltpu.make_async_copy(t_hbm, feats.at[0], load_sem.at[0])
    load_s = pltpu.make_async_copy(s_hbm, feats.at[1], load_sem.at[1])

    def load_p(j):
        cols = pl.ds(pl.multiple_of(j * TILE, TILE), TILE)
        return pltpu.make_async_copy(
            p_hbm.at[:, cols], q.at[j, pl.ds(0, width)], load_sem.at[2 + j]
        )

    load_t.start()
    for j in range(tiles):
        load_p(j).start()
    load_s.start()

    def group_send(src, dst, me, peers, ssem, rsem, n):
        for d, dev in enumerate(peers):
            rc(src(d), dst.at[me], ssem.at[d], rsem.at[me], dev).start()

    def group_wait(src, dst, me, peers, ssem, rsem, n):
        for d, dev in enumerate(peers):
            other = (me + d + 1) % n
            copy = rc(src(d), dst.at[other], ssem.at[d], rsem.at[other], dev)
            copy.wait_recv()
            copy.wait_send()

    load_t.wait()
    hi, lo = split(feats[0] * (LOG2E / (TEACHER_TEMP / STUDENT_TEMP)))
    thh[:, 0:width] = hi
    thh[:, width : 2 * width] = hi
    tl[...] = lo

    @pl.loop(0, tiles)
    def _(j):
        load_p(j).wait()
        ph, plo = split(q[j, 0:width, :] * (1.0 / STUDENT_TEMP))
        phl[j, 0:width, :] = ph
        phl[j, width : 2 * width, :] = plo
        scores = mm(thh[...], phl[j]) + mm(tl[...], phl[j, 0:width, :])
        top = jnp.max(scores, axis=0, keepdims=True)
        ex = jnp.exp2(scores - top)
        e[j] = ex
        total = jnp.sum(ex, axis=0, keepdims=True)
        for i in range(per):
            cola[pl.ds(per * j + i, 1), :] = top[:, LANES * i : LANES * (i + 1)]
            cola[pl.ds(per * (tiles + j) + i, 1), :] = total[:, LANES * i : LANES * (i + 1)]

    pl.semaphore_wait(barrier, len(smp_peers) + len(y_peers) + len(z_peers))

    def student(first, last):
        @pl.loop(first, last)
        def _(j):
            scores = mm(shh[...], phl[j]) + mm(sl[...], phl[j, 0:width, :])
            q[j] = scores
            for r in range(blocks):
                rs = slice(LANES * r, LANES * (r + 1))
                m = mx[rs, :]
                for i in range(per):
                    m = jnp.maximum(m, scores[rs, LANES * i : LANES * (i + 1)])
                mx[rs, :] = m

    def student_start():
        load_s.wait()
        sf = feats[1]
        shi, slo = split(sf * LOG2E)
        shh[:, 0:width] = shi
        shh[:, width : 2 * width] = shi
        sl[...] = slo
        mx[...] = jnp.full(mx.shape, -jnp.inf, f32)

    def student_transpose():
        keep = width // SN
        ht, lt = split((feats[1] * (1.0 / STUDENT_TEMP)).T)
        for core in range(2):
            for chip in range(XN):
                to = (core * XN + chip) * keep
                fr = (2 * chip + core) * keep
                st[0, to : to + keep, :] = ht[fr : fr + keep, :]
                st[1, to : to + keep, :] = lt[fr : fr + keep, :]

    def to_rows(ref, reduce, out, base):
        for r in range(blocks):
            rs = slice(LANES * r, LANES * (r + 1))
            out[base + r : base + r + 1, :] = reduce(ref[rs, :].T, axis=0, keepdims=True)

    def to_columns(v, out):
        for r in range(blocks):
            rs = slice(LANES * r, LANES * (r + 1))
            out[rs, :] = jnp.broadcast_to(v[r : r + 1, :], (LANES, LANES)).T

    def student_totals():
        to_rows(mx, jnp.max, stat, 0)
        to_columns(stat[0:blocks, :], ab)
        mx[...] = jnp.zeros(mx.shape, f32)

        @pl.loop(0, tiles)
        def _(j):
            for r in range(blocks):
                rs = slice(LANES * r, LANES * (r + 1))
                m = ab[rs, :]
                a = mx[rs, :]
                for i in range(per):
                    ls = slice(LANES * i, LANES * (i + 1))
                    v = jnp.exp2(q[j, rs, ls] - m)
                    q[j, rs, ls] = v
                    a = a + v
                mx[rs, :] = a

        to_rows(mx, jnp.sum, stat, blocks)

    def combine(ref):
        tops = [ref[k, 0:blocks, :] for k in range(ref.shape[0])]
        top = functools.reduce(jnp.maximum, tops)
        total = sum(ref[k, blocks : 2 * blocks, :] * jnp.exp2(tops[k] - top) for k in range(ref.shape[0]))
        return top, total

    def row_pass(it):
        acc[...] = jnp.zeros(acc.shape, f32)

        @pl.loop(0, tiles)
        def _(j):
            ws = [pscale[pl.ds(per * j + i, 1), :] for i in range(per)]
            fs = [peakf[pl.ds(per * j + i, 1), :] for i in range(per)] if it == 0 else None
            for r in range(blocks):
                rs = slice(LANES * r, LANES * (r + 1))
                a = acc[rs, :]
                for i in range(per):
                    ls = slice(LANES * i, LANES * (i + 1))
                    v = e[j, rs, ls]
                    if it == 0:
                        v = v * fs[i]
                        e[j, rs, ls] = v
                    a = a + v * ws[i]
                acc[rs, :] = a

        to_rows(acc, jnp.sum, rowm.at[it], 0)

    def row_start(it):
        row_y[it, pl.ds(y, 1)] = rowm[it : it + 1]
        group_send(lambda d: rowm.at[it], row_y.at[it], y, y_peers, rys_sem.at[it], ryr_sem.at[it], YN)

    def row_middle(it):
        group_wait(lambda d: rowm.at[it], row_y.at[it], y, y_peers, rys_sem.at[it], ryr_sem.at[it], YN)
        rowt[it] = sum(row_y[it, k] for k in range(YN))
        row_z[it, pl.ds(z, 1)] = rowt[it : it + 1]
        group_send(lambda d: rowt.at[it], row_z.at[it], z, z_peers, rzs_sem.at[it], rzr_sem.at[it], ZN)

    def row_end(it):
        group_wait(lambda d: rowt.at[it], row_z.at[it], z, z_peers, rzs_sem.at[it], rzr_sem.at[it], ZN)
        mass = sum(row_z[it, k] for k in range(ZN))
        to_columns(1.0 / mass, cb)

    def col_pass(it):
        @pl.loop(0, tiles)
        def _(j):
            for i in range(per):
                ls = slice(LANES * i, LANES * (i + 1))
                v = jnp.sum(e[j, :, ls] * cb[...], axis=0, keepdims=True)
                col[it, pl.ds(per * j + i, 1), :] = v

    def col_start(it):
        col_in[it, pl.ds(s, 1)] = col[it : it + 1]
        group_send(lambda d: col.at[it], col_in.at[it], s, smp_peers, cs_sem.at[it + 1], cr_sem.at[it + 1], SN)

    def col_end(it):
        group_wait(lambda d: col.at[it], col_in.at[it], s, smp_peers, cs_sem.at[it + 1], cr_sem.at[it + 1], SN)
        pscale[...] = 1.0 / sum(col_in[it, k] for k in range(SN))

    half = per * tiles
    cola_in[pl.ds(s, 1)] = cola[...][None]
    group_send(lambda d: cola, cola_in, s, smp_peers, cs_sem.at[0], cr_sem.at[0], SN)
    student_start()
    student(0, tiles // 4)
    group_wait(lambda d: cola, cola_in, s, smp_peers, cs_sem.at[0], cr_sem.at[0], SN)
    tops = [cola_in[k, 0:half, :] for k in range(SN)]
    top = functools.reduce(jnp.maximum, tops)
    pscale[...] = 1.0 / sum(cola_in[k, half : 2 * half, :] * jnp.exp2(tops[k] - top) for k in range(SN))
    peakf[...] = jnp.exp2(cola[0:half, :] - top)

    row_pass(0)
    row_start(0)
    student(tiles // 4, tiles // 2)
    row_middle(0)
    student(tiles // 2, 3 * tiles // 4)
    row_end(0)
    col_pass(0)
    col_start(0)
    student(3 * tiles // 4, tiles)
    col_end(0)

    row_pass(1)
    row_start(1)
    student_totals()
    stat_y[pl.ds(y, 1)] = stat[...][None]
    group_send(lambda d: stat, stat_y, y, y_peers, sts_sem.at[0], str_sem.at[0], YN)
    row_middle(1)
    student_transpose()
    row_end(1)
    col_pass(1)
    col_start(1)
    group_wait(lambda d: stat, stat_y, y, y_peers, sts_sem.at[0], str_sem.at[0], YN)
    top, total = combine(stat_y)
    stat_t[0:blocks, :] = top
    stat_t[blocks : 2 * blocks, :] = total
    stat_z[pl.ds(z, 1)] = stat_t[...][None]
    group_send(lambda d: stat_t, stat_z, z, z_peers, sts_sem.at[1], str_sem.at[1], ZN)
    gfacc[...] = jnp.zeros(gfacc.shape, f32)
    col_end(1)

    row_pass(2)
    row_start(2)
    group_wait(lambda d: stat_t, stat_z, z, z_peers, sts_sem.at[1], str_sem.at[1], ZN)
    top, total = combine(stat_z)
    to_columns(jnp.exp2(stat[0:blocks, :] - top) / total, ab)
    row_middle(2)
    row_end(2)

    @pl.loop(0, tiles)
    def _(j):
        for i in range(per):
            ls = slice(LANES * i, LANES * (i + 1))
            w = pscale[pl.ds(per * j + i, 1), :]
            d = q[j, :, ls] * ab[...] - (cb[...] * e[j, :, ls]) * w
            dhi, dlo = split(d)
            dh[j, :, ls] = dhi
            dl[j, :, ls] = dlo
        gfacc[...] += mm_t(dh[j], phl[j])
        gfacc[:, 0:width] += mm_t(dl[j], phl[j, 0:width, :])

    part = rows // YN
    piece = part // ZN
    for k in range(YN):
        rs = slice(k * part, (k + 1) * part)
        gfs[k] = gfacc[rs, 0:width] + gfacc[rs, width : 2 * width]

    def ypeer(d):
        return (y + d + 1) % YN

    def zpeer(d):
        return (z + d + 1) % ZN

    def gf_a():
        group_send(lambda d: gfs.at[ypeer(d)], gfy, y, y_peers, gs_sem.at[0], gr_sem.at[0], YN)

    def gf_b():
        group_wait(lambda d: gfs.at[ypeer(d)], gfy, y, y_peers, gs_sem.at[0], gr_sem.at[0], YN)
        gfy[pl.ds(y, 1)] = gfs[pl.ds(y, 1)]
        v = sum(gfy[k] for k in range(YN))
        for k in range(ZN):
            gft[k] = v[k * piece : (k + 1) * piece]
        group_send(lambda d: gft.at[zpeer(d)], gfz, z, z_peers, gs_sem.at[1], gr_sem.at[1], ZN)

    def gf_c():
        group_wait(lambda d: gft.at[zpeer(d)], gfz, z, z_peers, gs_sem.at[1], gr_sem.at[1], ZN)
        gfz[pl.ds(z, 1)] = gft[pl.ds(z, 1)]
        gfz2[pl.ds(z, 1)] = sum(gfz[k] for k in range(ZN))[None]
        group_send(lambda d: gfz2.at[z], gfz2, z, z_peers, gs_sem.at[2], gr_sem.at[2], ZN)

    def gf_d():
        group_wait(lambda d: gfz2.at[z], gfz2, z, z_peers, gs_sem.at[2], gr_sem.at[2], ZN)
        mine = pl.multiple_of(y * part, part)
        for k in range(ZN):
            gf_out[pl.ds(pl.multiple_of(mine + k * piece, piece), piece), :] = gfz2[k]
        for d, dev in enumerate(y_peers):
            block = gf_out.at[pl.ds(mine, part)]
            rc(block, block, gs_sem.at[3, d], gr_sem.at[3, y], dev).start()

    def gf_e():
        mine = pl.multiple_of(y * part, part)
        for d, dev in enumerate(y_peers):
            block = gf_out.at[pl.ds(mine, part)]
            theirs = gf_out.at[pl.ds(pl.multiple_of(ypeer(d) * part, part), part)]
            copy = rc(block, theirs, gs_sem.at[3, d], gr_sem.at[3, ypeer(d)], dev)
            copy.wait_recv()
            copy.wait_send()

    gf_a()

    keep = width // SN
    hk = keep // 2
    mine = pl.multiple_of(c * (width // 2), width // 2)
    other = pl.multiple_of((1 - c) * (width // 2), width // 2)
    across = pl.multiple_of(((x + 2) % XN) * keep, keep)
    ahead = pl.multiple_of(((x + 1) % XN) * keep, keep)
    behind = pl.multiple_of(((x + XN - 1) % XN) * keep, keep)
    here = pl.multiple_of(x * keep, keep)

    def core_copy(t):
        return rc(e.at[t, pl.ds(other, width // 2)], cr.at[t], ks_sem.at[t], kr_sem.at[t], sibling)

    def x_copy(t, k):
        row, dst, dev = [
            (across, xa.at[t, 0], right),
            (across + hk, xa.at[t, 1], left),
            (ahead + hk, xb.at[t, 0, pl.ds(hk, hk)], right),
            (behind, xb.at[t, 1, pl.ds(0, hk)], left),
            (ahead, xb.at[t, 0, pl.ds(0, hk)], right),
            (behind + hk, xb.at[t, 1, pl.ds(hk, hk)], left),
        ][k]
        src = cr.at[t, pl.ds(pl.multiple_of(row, 8), hk)]
        return rc(src, dst, xs_sem.at[t, k], xr_sem.at[t, k], dev)

    lag_core, lag_a, lag_b = 1, 3, 5

    @pl.loop(0, tiles + lag_b)
    def _(i):
        @pl.when(i < tiles)
        def _():
            d = dh[i]
            e[i, 0:width, :] = mm(st[0], d) + mm(st[1], d) + mm(st[0], dl[i])
            core_copy(i).start()

        @pl.when((i >= lag_core) & (i < tiles + lag_core))
        def _():
            t = i - lag_core
            core_copy(t).wait_recv()
            cr[t] = cr[t] + e[t, pl.ds(mine, width // 2), :]
            for k in range(4):
                x_copy(t, k).start()

        @pl.when((i >= lag_a) & (i < tiles + lag_a))
        def _():
            t = i - lag_a
            x_copy(t, 0).wait_recv()
            x_copy(t, 1).wait_recv()
            a = pl.ds(pl.multiple_of(ahead, 8), hk)
            cr[t, a, :] = cr[t, a, :] + xa[t, 0]
            b = pl.ds(pl.multiple_of(behind + hk, 8), hk)
            cr[t, b, :] = cr[t, b, :] + xa[t, 1]
            x_copy(t, 4).start()
            x_copy(t, 5).start()

        @pl.when(i >= lag_b)
        def _():
            t = i - lag_b
            for k in range(2, 6):
                x_copy(t, k).wait_recv()
            cols = pl.ds(pl.multiple_of(t * TILE, TILE), TILE)
            gp_out[:, cols] = cr[t, pl.ds(here, keep), :] + xb[t, 0] + xb[t, 1]
            core_copy(t).wait_send()
            for k in range(6):
                x_copy(t, k).wait_send()

        @pl.when(i == 5)
        def _():
            gf_b()

        @pl.when(i == 7)
        def _():
            gf_c()

        @pl.when(i == 9)
        def _():
            gf_d()

    gf_e()


def local(SN, PN, teacher_feats, student_feats, prototypes):
    rows, width = teacher_feats.shape
    protos = prototypes.shape[1]
    tiles = protos // TILE
    half = protos // LANES
    blocks = rows // LANES
    ZN = PN // YN
    part = rows // YN
    piece = part // ZN
    V = pltpu.VMEM
    DMA = pltpu.SemaphoreType.DMA
    scratch = [
        V((2, rows, width), f32),
        V((rows, 2 * width), bf16),
        V((rows, width), bf16),
        V((rows, 2 * width), bf16),
        V((rows, width), bf16),
        V((2, width, rows), bf16),
        V((tiles, 2 * width, TILE), bf16),
        V((tiles, rows, TILE), f32),
        V((tiles, rows, TILE), f32),
        V((tiles, rows, TILE), bf16),
        V((tiles, rows, TILE), bf16),
        V((2 * half, LANES), f32),
        V((SN, 2 * half, LANES), f32),
        V((ITERS - 1, half, LANES), f32),
        V((ITERS - 1, SN, half, LANES), f32),
        V((half, LANES), f32),
        V((half, LANES), f32),
        V((rows, LANES), f32),
        V((rows, LANES), f32),
        V((rows, LANES), f32),
        V((rows, LANES), f32),
        V((ITERS, blocks, LANES), f32),
        V((ITERS, YN, blocks, LANES), f32),
        V((ITERS, ZN, blocks, LANES), f32),
        V((ITERS, blocks, LANES), f32),
        V((2 * blocks, LANES), f32),
        V((YN, 2 * blocks, LANES), f32),
        V((2 * blocks, LANES), f32),
        V((ZN, 2 * blocks, LANES), f32),
        V((rows, 2 * width), f32),
        V((YN, part, width), f32),
        V((YN, part, width), f32),
        V((ZN, piece, width), f32),
        V((ZN, piece, width), f32),
        V((ZN, piece, width), f32),
        V((tiles, width // 2, TILE), f32),
        V((tiles, 2, width // SN // 2, TILE), f32),
        V((tiles, 2, width // SN, TILE), f32),
        DMA((2 + tiles,)),
        DMA((ITERS, SN - 1)),
        DMA((ITERS, SN)),
        DMA((ITERS, YN - 1)),
        DMA((ITERS, YN)),
        DMA((ITERS, ZN - 1)),
        DMA((ITERS, ZN)),
        DMA((2, ZN - 1)),
        DMA((2, ZN)),
        DMA((4, ZN - 1)),
        DMA((4, ZN)),
        DMA((tiles,)),
        DMA((tiles,)),
        DMA((tiles, 6)),
        DMA((tiles, 6)),
    ]
    flops = 2 * rows * width * protos
    return pl.pallas_call(
        functools.partial(kernel, SN, PN),
        out_shape=(
            jax.ShapeDtypeStruct((rows, width), f32),
            jax.ShapeDtypeStruct((width // SN, protos), f32),
        ),
        in_specs=[pl.BlockSpec(memory_space=pl.ANY)] * 3,
        out_specs=(pl.BlockSpec(memory_space=pltpu.VMEM), pl.BlockSpec(memory_space=pltpu.VMEM)),
        scratch_shapes=scratch,
        compiler_params=pltpu.CompilerParams(
            collective_id=0, has_side_effects=True, vmem_limit_bytes=62 * 1024 * 1024
        ),
        cost_estimate=pl.CostEstimate(
            flops=12 * flops, bytes_accessed=4 * width * (protos + 4 * rows), transcendentals=2 * rows * protos
        ),
    )(teacher_feats, student_feats, prototypes)


def solution(mesh):
    SN, PN = mesh.shape["smp"], mesh.shape["proto"]
    in_specs = (P("smp", None), P("smp", None), P(None, "proto"))
    out_specs = (P("smp", None), P("smp", "proto"))
    return jax.shard_map(
        functools.partial(local, SN, PN), mesh=mesh, in_specs=in_specs, out_specs=out_specs, check_vma=False
    )
```

```python
import functools

import jax
import jax.numpy as jnp
from jax import lax
from jax.experimental import pallas as pl
from jax.experimental.pallas import tpu as pltpu
from jax.sharding import PartitionSpec as P

ITERS = 3
TEACHER_TEMP = 0.07
STUDENT_TEMP = 0.1
LOG2E = 1.4426950408889634

YN = 4
TILE = 512
LANES = 128
MESH = pl.DeviceIdType.MESH
f32 = jnp.float32
bf16 = jnp.bfloat16


def mm(a, b):
    return jnp.dot(a, b, preferred_element_type=f32)


def mm_t(a, b):
    return lax.dot_general(a, b, (((1,), (1,)), ((), ())), preferred_element_type=f32)


def split(v):
    hi = v.astype(bf16)
    return hi, (v - hi.astype(f32)).astype(bf16)


def kernel(
    SN,
    PN,
    t_hbm,
    s_hbm,
    p_hbm,
    gf_out,
    gp_out,
    feats,
    thh,
    tl,
    shh,
    sl,
    st,
    phl,
    e,
    q,
    dh,
    dl,
    cola,
    cola_in,
    col,
    col_in,
    pscale,
    peakf,
    acc,
    mx,
    cb,
    ab,
    rowm,
    row_in,
    stat,
    stat_in,
    gfacc,
    gfs,
    gya,
    gyb,
    gfz,
    gft,
    gfz2,
    gfo,
    cr,
    xa,
    xb,
    gpo,
    load_sem,
    cs_sem,
    cr_sem,
    rs_sem,
    rr_sem,
    st_sem,
    ys_sem,
    yr_sem,
    zs_sem,
    zr_sem,
    ks_sem,
    kr_sem,
    xs_sem,
    xr_sem,
    out_sem,
):
    ZN = PN // YN
    XN = SN // 2
    rows, width = t_hbm.shape
    tiles = p_hbm.shape[1] // TILE
    per = TILE // LANES
    blocks = rows // LANES
    s = lax.axis_index("smp")
    p = lax.axis_index("proto")
    x = s // 2
    c = s % 2
    z = p // YN
    y = p % YN
    sibling = (2 * x + 1 - c, p)
    right = (2 * ((x + 1) % XN) + c, p)
    left = (2 * ((x + XN - 1) % XN) + c, p)
    y_right = (s, z * YN + (y + 1) % YN)
    y_left = (s, z * YN + (y + YN - 1) % YN)

    def far(d, n):
        return min(d, n - d)

    offsets = sorted(((dx, dc) for dx in range(XN) for dc in range(2)), key=lambda o: -far(o[0], XN))
    smp_peers = [2 * ((x + dx) % XN) + (c + dc) % 2 for dx, dc in offsets if dx or dc]
    smp_group = (s, SN, [(k, (k, p)) for k in smp_peers])
    offsets = sorted(((dz, dy) for dz in range(ZN) for dy in range(YN)), key=lambda o: -far(o[0], ZN) - far(o[1], YN))
    row_peers = [((z + dz) % ZN) * YN + (y + dy) % YN for dz, dy in offsets if dz or dy]
    row_group = (p, PN, [(k, (s, k)) for k in row_peers])
    z_peers = [(z + dz) % ZN for dz in sorted(range(1, ZN), key=lambda d: -far(d, ZN))]
    z_group = (z, ZN, [(k, (s, k * YN + y)) for k in z_peers])

    def rc(src, dst, ss, rs, dev):
        return pltpu.make_async_remote_copy(
            src_ref=src, dst_ref=dst, send_sem=ss, recv_sem=rs, device_id=dev, device_id_type=MESH
        )

    barrier = pltpu.get_barrier_semaphore()
    for _, dev in smp_group[2] + row_group[2]:
        pl.semaphore_signal(barrier, inc=1, device_id=dev, device_id_type=MESH)

    load_t = pltpu.make_async_copy(t_hbm, feats.at[0], load_sem.at[0])
    load_s = pltpu.make_async_copy(s_hbm, feats.at[1], load_sem.at[1])

    def load_p(j):
        cols = pl.ds(pl.multiple_of(j * TILE, TILE), TILE)
        return pltpu.make_async_copy(
            p_hbm.at[:, cols], q.at[j, pl.ds(0, width)], load_sem.at[2 + j]
        )

    load_t.start()
    for j in range(tiles):
        load_p(j).start()
    load_s.start()

    def group_send(src, dst, group, ssem, rsem):
        me, n, peers = group
        for k, dev in peers:
            rc(src(k), dst.at[me], ssem, rsem, dev).start()

    def group_wait(dst, group, ssem, rsem):
        me, n, peers = group
        blocks = dst.at[pl.ds(0, n - 1)]
        copy = rc(blocks, blocks, ssem, rsem, peers[0][1])
        copy.wait_recv()
        copy.wait_send()

    load_t.wait()
    hi, lo = split(feats[0] * (LOG2E / (TEACHER_TEMP / STUDENT_TEMP)))
    thh[:, 0:width] = hi
    thh[:, width : 2 * width] = hi
    tl[...] = lo

    @pl.loop(0, tiles)
    def _(j):
        load_p(j).wait()
        ph, plo = split(q[j, 0:width, :] * (1.0 / STUDENT_TEMP))
        phl[j, 0:width, :] = ph
        phl[j, width : 2 * width, :] = plo
        scores = mm(thh[...], phl[j]) + mm(tl[...], phl[j, 0:width, :])
        top = jnp.max(scores, axis=0, keepdims=True)
        ex = jnp.exp2(scores - top)
        e[j] = ex
        total = jnp.sum(ex, axis=0, keepdims=True)
        for i in range(per):
            cola[pl.ds(per * j + i, 1), :] = top[:, LANES * i : LANES * (i + 1)]
            cola[pl.ds(per * (tiles + j) + i, 1), :] = total[:, LANES * i : LANES * (i + 1)]

    pl.semaphore_wait(barrier, len(smp_peers) + len(row_peers))

    def student(first, last):
        @pl.loop(first, last)
        def _(j):
            scores = mm(shh[...], phl[j]) + mm(sl[...], phl[j, 0:width, :])
            q[j] = scores
            for r in range(blocks):
                rs = slice(LANES * r, LANES * (r + 1))
                m = mx[rs, :]
                for i in range(per):
                    m = jnp.maximum(m, scores[rs, LANES * i : LANES * (i + 1)])
                mx[rs, :] = m

    def student_start():
        load_s.wait()
        sf = feats[1]
        shi, slo = split(sf * LOG2E)
        shh[:, 0:width] = shi
        shh[:, width : 2 * width] = shi
        sl[...] = slo
        mx[...] = jnp.full(mx.shape, -jnp.inf, f32)

    def student_transpose():
        keep = width // SN
        ht, lt = split((feats[1] * (1.0 / STUDENT_TEMP)).T)
        for core in range(2):
            for chip in range(XN):
                to = (core * XN + chip) * keep
                fr = (2 * chip + core) * keep
                st[0, to : to + keep, :] = ht[fr : fr + keep, :]
                st[1, to : to + keep, :] = lt[fr : fr + keep, :]

    def to_rows(ref, reduce, out, base):
        for r in range(blocks):
            rs = slice(LANES * r, LANES * (r + 1))
            out[base + r : base + r + 1, :] = reduce(ref[rs, :].T, axis=0, keepdims=True)

    def to_columns(v, out):
        for r in range(blocks):
            rs = slice(LANES * r, LANES * (r + 1))
            out[rs, :] = jnp.broadcast_to(v[r : r + 1, :], (LANES, LANES)).T

    def student_totals():
        to_rows(mx, jnp.max, stat, 0)
        to_columns(stat[0:blocks, :], ab)
        mx[...] = jnp.zeros(mx.shape, f32)

        @pl.loop(0, tiles)
        def _(j):
            for r in range(blocks):
                rs = slice(LANES * r, LANES * (r + 1))
                m = ab[rs, :]
                a = mx[rs, :]
                for i in range(per):
                    ls = slice(LANES * i, LANES * (i + 1))
                    v = jnp.exp2(q[j, rs, ls] - m)
                    q[j, rs, ls] = v
                    a = a + v
                mx[rs, :] = a

        to_rows(mx, jnp.sum, stat, blocks)

    def row_pass(it):
        acc[...] = jnp.zeros(acc.shape, f32)

        @pl.loop(0, tiles)
        def _(j):
            ws = [pscale[pl.ds(per * j + i, 1), :] for i in range(per)]
            fs = [peakf[pl.ds(per * j + i, 1), :] for i in range(per)] if it == 0 else None
            for r in range(blocks):
                rs = slice(LANES * r, LANES * (r + 1))
                a = acc[rs, :]
                for i in range(per):
                    ls = slice(LANES * i, LANES * (i + 1))
                    v = e[j, rs, ls]
                    if it == 0:
                        v = v * fs[i]
                        e[j, rs, ls] = v
                    a = a + v * ws[i]
                acc[rs, :] = a

        to_rows(acc, jnp.sum, rowm.at[it], 0)

    def row_start(it):
        row_in[it, pl.ds(p, 1)] = rowm[it : it + 1]
        group_send(lambda k: rowm.at[it], row_in.at[it], row_group, rs_sem.at[it], rr_sem.at[it])

    def row_end(it):
        group_wait(row_in.at[it], row_group, rs_sem.at[it], rr_sem.at[it])
        mass = sum(row_in[it, k] for k in range(PN))
        to_columns(1.0 / mass, cb)

    def col_pass(it):
        @pl.loop(0, tiles)
        def _(j):
            for i in range(per):
                ls = slice(LANES * i, LANES * (i + 1))
                v = jnp.sum(e[j, :, ls] * cb[...], axis=0, keepdims=True)
                col[it, pl.ds(per * j + i, 1), :] = v

    def col_start(it):
        col_in[it, pl.ds(s, 1)] = col[it : it + 1]
        group_send(lambda k: col.at[it], col_in.at[it], smp_group, cs_sem.at[it + 1], cr_sem.at[it + 1])

    def col_end(it):
        group_wait(col_in.at[it], smp_group, cs_sem.at[it + 1], cr_sem.at[it + 1])
        pscale[...] = 1.0 / sum(col_in[it, k] for k in range(SN))

    keep = width // SN
    hk = keep // 2
    mine = pl.multiple_of(c * (width // 2), width // 2)
    other = pl.multiple_of((1 - c) * (width // 2), width // 2)
    across = pl.multiple_of(((x + 2) % XN) * keep, keep)
    ahead = pl.multiple_of(((x + 1) % XN) * keep, keep)
    behind = pl.multiple_of(((x + XN - 1) % XN) * keep, keep)
    here = pl.multiple_of(x * keep, keep)

    def core_copy(t):
        return rc(e.at[t, pl.ds(other, width // 2)], cr.at[t], ks_sem.at[t], kr_sem.at[t], sibling)

    def x_copy(t, k):
        row, dst, dev = [
            (across, xa.at[t, 0], right),
            (across + hk, xa.at[t, 1], left),
            (ahead + hk, xb.at[t, 0, pl.ds(hk, hk)], right),
            (behind, xb.at[t, 1, pl.ds(0, hk)], left),
            (ahead, xb.at[t, 0, pl.ds(0, hk)], right),
            (behind + hk, xb.at[t, 1, pl.ds(hk, hk)], left),
        ][k]
        src = cr.at[t, pl.ds(pl.multiple_of(row, 8), hk)]
        return rc(src, dst, xs_sem.at[t, k], xr_sem.at[t, k], dev)

    def out_copy(t):
        cols = pl.ds(pl.multiple_of(t * TILE, TILE), TILE)
        return pltpu.make_async_copy(gpo.at[t], gp_out.at[:, cols], out_sem.at[t])

    def gp_terms(t):
        d = dh[t]
        e[t, 0:width, :] = mm(st[0], d) + mm(st[1], d) + mm(st[0], dl[t])
        core_copy(t).start()

    def gp_core(t):
        core_copy(t).wait_recv()
        cr[t] = cr[t] + e[t, pl.ds(mine, width // 2), :]
        x_copy(t, 0).start()
        x_copy(t, 1).start()

    def gp_relay(t):
        x_copy(t, 0).wait_recv()
        x_copy(t, 1).wait_recv()
        a = pl.ds(pl.multiple_of(ahead, 8), hk)
        cr[t, a, :] = cr[t, a, :] + xa[t, 0]
        b = pl.ds(pl.multiple_of(behind + hk, 8), hk)
        cr[t, b, :] = cr[t, b, :] + xa[t, 1]
        for k in range(2, 6):
            x_copy(t, k).start()

    def gp_end(t):
        for k in range(2, 6):
            x_copy(t, k).wait_recv()
        gpo[t] = cr[t, pl.ds(here, keep), :] + xb[t, 0] + xb[t, 1]
        out_copy(t).start()
        core_copy(t).wait_send()
        for k in range(6):
            x_copy(t, k).wait_send()

    part = rows // 2
    chunk = part // YN
    hc = chunk // 2
    piece = chunk // ZN

    def chunk_at(r, d, low, size):
        return pl.ds(pl.multiple_of((r % 2) * part + ((y + d) % YN) * chunk + low, 8), size)

    def y_copy(r, k):
        d, low, dst, dev = [
            (2, 0, gya.at[r, 0], y_right),
            (2, hc, gya.at[r, 1], y_left),
            (1, hc, gyb.at[r, 0, pl.ds(hc, hc)], y_right),
            (YN - 1, 0, gyb.at[r, 1, pl.ds(0, hc)], y_left),
            (1, 0, gyb.at[r, 0, pl.ds(0, hc)], y_right),
            (YN - 1, hc, gyb.at[r, 1, pl.ds(hc, hc)], y_left),
        ][k]
        return rc(gfs.at[r // 2, chunk_at(r, d, low, hc)], dst, ys_sem.at[r, k], yr_sem.at[r, k], dev)

    def y_gather(r, k):
        d, low, size, dev = [
            (0, 0, chunk, y_right),
            (0, 0, chunk, y_left),
            (YN - 1, 0, hc, y_right),
            (1, hc, hc, y_left),
        ][k]
        src = gfo.at[chunk_at(r, d, low, size)]
        return rc(src, src, ys_sem.at[r, 6 + k], yr_sem.at[r, 6 + k], dev)

    def y_arrive(r, k):
        d, low, size = [(YN - 1, 0, chunk), (1, 0, chunk), (2, 0, hc), (2, hc, hc)][k]
        dst = gfo.at[chunk_at(r, d, low, size)]
        rc(dst, dst, ys_sem.at[r, 6 + k], yr_sem.at[r, 6 + k], y_right).wait_recv()

    def gf_a(r):
        for k in range(4):
            y_copy(r, k).start()

    def gf_b(r):
        for k in range(2):
            y_copy(r, k).wait_recv()
        a = chunk_at(r, 1, 0, hc)
        gfs[r // 2, a, :] = gfs[r // 2, a, :] + gya[r, 0]
        b = chunk_at(r, YN - 1, hc, hc)
        gfs[r // 2, b, :] = gfs[r // 2, b, :] + gya[r, 1]
        y_copy(r, 4).start()
        y_copy(r, 5).start()

    def gf_c(r):
        for k in range(2, 6):
            y_copy(r, k).wait_recv()
        for k in range(ZN):
            rs = slice(k * piece, (k + 1) * piece)
            own = gfs[r // 2, chunk_at(r, 0, k * piece, piece), :]
            gft[r, k] = own + gyb[r, 0, rs, :] + gyb[r, 1, rs, :]
        group_send(lambda k: gft.at[r, k], gfz.at[r], z_group, zs_sem.at[r], zr_sem.at[r])

    def gf_d(r):
        group_wait(gfz.at[r], z_group, zs_sem.at[r], zr_sem.at[r])
        gfz[r, pl.ds(z, 1)] = gft[r, pl.ds(z, 1)]
        if r < 2:
            targets = sum(gfz[r, k] for k in range(ZN))
            probs = sum(gfz[r + 2, k] for k in range(ZN))
            scale = cb[chunk_at(r, 0, z * piece, piece), :]
            scale = jnp.concatenate([scale] * (width // LANES), axis=1)
            gfz2[r, pl.ds(z, 1)] = (probs - scale * targets)[None]
            group_send(lambda k: gfz2.at[r, z], gfz2.at[r], z_group, zs_sem.at[4 + r], zr_sem.at[4 + r])

    def gf_e(r):
        group_wait(gfz2.at[r], z_group, zs_sem.at[4 + r], zr_sem.at[4 + r])
        for k in range(ZN):
            gfo[chunk_at(r, 0, k * piece, piece), :] = gfz2[r, k]
        y_gather(r, 0).start()
        y_gather(r, 1).start()

    def gf_f(r):
        y_arrive(r, 0)
        y_arrive(r, 1)
        y_gather(r, 2).start()
        y_gather(r, 3).start()

    def gf_copy(r):
        rs = pl.ds(r * part, part)
        return pltpu.make_async_copy(gfo.at[rs], gf_out.at[rs], out_sem.at[tiles + r])

    def gf_g(r):
        y_arrive(r, 2)
        y_arrive(r, 3)
        gf_copy(r).start()
        for k in range(6):
            y_copy(r, k).wait_send()
            y_copy(r + 2, k).wait_send()
        for k in range(4):
            y_gather(r, k).wait_send()

    def feat_terms(j, which, rs):
        gfacc[which, rs, :] += mm_t(dh[j, rs, :], phl[j])
        gfacc[which, rs, 0:width] += mm_t(dl[j, rs, :], phl[j, 0:width, :])

    everything = slice(0, rows)
    halves = [slice(0, part), slice(part, rows)]

    def probs_terms():
        gfacc[...] = jnp.zeros(gfacc.shape, f32)

        @pl.loop(0, tiles)
        def _(j):
            hi, lo = split(q[j])
            dh[j] = hi
            dl[j] = lo
            feat_terms(j, 1, everything)

    def probs_sum():
        for k in range(width // LANES):
            ls = slice(LANES * k, LANES * (k + 1))
            us = slice(width + LANES * k, width + LANES * (k + 1))
            gfs[1, :, ls] = (gfacc[1, :, ls] + gfacc[1, :, us]) * ab[...]
        gf_a(2)
        gf_a(3)

    def mass_terms(h):
        @pl.loop(0, tiles)
        def _(j):
            if h == 0:
                for k in range(per):
                    ls = slice(LANES * k, LANES * (k + 1))
                    hi, lo = split(e[j, :, ls] * pscale[pl.ds(per * j + k, 1), :])
                    dh[j, :, ls] = hi
                    dl[j, :, ls] = lo
            feat_terms(j, 0, halves[h])

        rs = halves[h]
        gfs[0, rs, :] = gfacc[0, rs, 0:width] + gfacc[0, rs, width : 2 * width]
        gf_a(h)

    half = per * tiles
    cola_in[pl.ds(s, 1)] = cola[...][None]
    group_send(lambda k: cola, cola_in, smp_group, cs_sem.at[0], cr_sem.at[0])
    student_start()
    student(0, tiles // 2)
    group_wait(cola_in, smp_group, cs_sem.at[0], cr_sem.at[0])
    tops = [cola_in[k, 0:half, :] for k in range(SN)]
    top = functools.reduce(jnp.maximum, tops)
    pscale[...] = 1.0 / sum(cola_in[k, half : 2 * half, :] * jnp.exp2(tops[k] - top) for k in range(SN))
    peakf[...] = jnp.exp2(cola[0:half, :] - top)

    row_pass(0)
    row_start(0)
    student(tiles // 2, tiles)
    student_totals()
    row_end(0)
    col_pass(0)
    col_start(0)
    stat_in[pl.ds(p, 1)] = stat[...][None]
    group_send(lambda k: stat, stat_in, row_group, st_sem.at[0], st_sem.at[1])
    student_transpose()
    col_end(0)

    row_pass(1)
    row_start(1)
    probs_terms()
    group_wait(stat_in, row_group, st_sem.at[0], st_sem.at[1])
    tops = [stat_in[k, 0:blocks, :] for k in range(PN)]
    top = functools.reduce(jnp.maximum, tops)
    total = sum(stat_in[k, blocks : 2 * blocks, :] * jnp.exp2(tops[k] - top) for k in range(PN))
    to_columns(jnp.exp2(stat[0:blocks, :] - top) / total, ab)
    row_end(1)
    col_pass(1)
    col_start(1)
    probs_sum()
    col_end(1)

    row_pass(2)
    row_start(2)
    gf_b(2)
    gf_b(3)
    mass_terms(0)
    mass_terms(1)
    row_end(2)

    lag_core, lag_relay, lag_end = 2, 6, 10
    at = {
        0: [(gf_c, 2), (gf_c, 3), (gf_b, 0)],
        3: [(gf_b, 1)],
        4: [(gf_c, 0)],
        6: [(gf_c, 1)],
        8: [(gf_d, 2), (gf_d, 3)],
        9: [(gf_d, 0)],
        10: [(gf_d, 1)],
        12: [(gf_e, 0)],
        13: [(gf_e, 1)],
        14: [(gf_f, 0)],
        15: [(gf_f, 1)],
        16: [(gf_g, 0)],
        17: [(gf_g, 1)],
    }

    @pl.loop(0, tiles + lag_end)
    def _(i):
        @pl.when(i < tiles)
        def _():
            for k in range(per):
                ls = slice(LANES * k, LANES * (k + 1))
                w = pscale[pl.ds(per * i + k, 1), :]
                d = q[i, :, ls] * ab[...] - (cb[...] * e[i, :, ls]) * w
                dhi, dlo = split(d)
                dh[i, :, ls] = dhi
                dl[i, :, ls] = dlo
            gp_terms(i)

        @pl.when((i >= lag_core) & (i < tiles + lag_core))
        def _():
            gp_core(i - lag_core)

        @pl.when((i >= lag_relay) & (i < tiles + lag_relay))
        def _():
            gp_relay(i - lag_relay)

        for when, todo in at.items():

            @pl.when(i == when)
            def _(todo=todo):
                for f, h in todo:
                    f(h)

        @pl.when(i >= lag_end)
        def _():
            gp_end(i - lag_end)

    for t in range(tiles):
        out_copy(t).wait()
    for h in range(2):
        gf_copy(h).wait()


def finish(gf_in, gp_in, gf_out, gp_out, gf_mid, gp_mid, sem):
    copies = []
    for k, (src, mid, dst) in enumerate(((gf_in, gf_mid, gf_out), (gp_in, gp_mid, gp_out))):
        n = src.shape[0] // 2
        for h in range(2):
            rs = pl.ds(h * n, n)
            first = pltpu.make_async_copy(src.at[rs], mid.at[rs], sem.at[0, 2 * k + h])
            second = pltpu.make_async_copy(mid.at[rs], dst.at[rs], sem.at[1, 2 * k + h])
            first.start()
            copies.append((first, second))
    for first, second in copies:
        first.wait()
        second.start()
    for first, second in copies:
        second.wait()


def local(SN, PN, teacher_feats, student_feats, prototypes):
    rows, width = teacher_feats.shape
    protos = prototypes.shape[1]
    tiles = protos // TILE
    half = protos // LANES
    blocks = rows // LANES
    ZN = PN // YN
    chunk = rows // 2 // YN
    piece = chunk // ZN
    V = pltpu.VMEM
    DMA = pltpu.SemaphoreType.DMA
    scratch = [
        V((2, rows, width), f32),
        V((rows, 2 * width), bf16),
        V((rows, width), bf16),
        V((rows, 2 * width), bf16),
        V((rows, width), bf16),
        V((2, width, rows), bf16),
        V((tiles, 2 * width, TILE), bf16),
        V((tiles, rows, TILE), f32),
        V((tiles, rows, TILE), f32),
        V((tiles, rows, TILE), bf16),
        V((tiles, rows, TILE), bf16),
        V((2 * half, LANES), f32),
        V((SN, 2 * half, LANES), f32),
        V((ITERS - 1, half, LANES), f32),
        V((ITERS - 1, SN, half, LANES), f32),
        V((half, LANES), f32),
        V((half, LANES), f32),
        V((rows, LANES), f32),
        V((rows, LANES), f32),
        V((rows, LANES), f32),
        V((rows, LANES), f32),
        V((ITERS, blocks, LANES), f32),
        V((ITERS, PN, blocks, LANES), f32),
        V((2 * blocks, LANES), f32),
        V((PN, 2 * blocks, LANES), f32),
        V((2, rows, 2 * width), f32),
        V((2, rows, width), f32),
        V((4, 2, chunk // 2, width), f32),
        V((4, 2, chunk, width), f32),
        V((4, ZN, piece, width), f32),
        V((4, ZN, piece, width), f32),
        V((2, ZN, piece, width), f32),
        V((rows, width), f32),
        V((tiles, width // 2, TILE), f32),
        V((tiles, 2, width // SN // 2, TILE), f32),
        V((tiles, 2, width // SN, TILE), f32),
        V((tiles, width // SN, TILE), f32),
        DMA((2 + tiles,)),
        DMA((ITERS,)),
        DMA((ITERS,)),
        DMA((ITERS,)),
        DMA((ITERS,)),
        DMA((2,)),
        DMA((4, 10)),
        DMA((4, 10)),
        DMA((6,)),
        DMA((6,)),
        DMA((tiles,)),
        DMA((tiles,)),
        DMA((tiles, 6)),
        DMA((tiles, 6)),
        DMA((tiles + 2,)),
    ]
    flops = 2 * rows * width * protos
    shapes = (
        jax.ShapeDtypeStruct((rows, width), f32),
        jax.ShapeDtypeStruct((width // SN, protos), f32),
    )
    outs = pl.pallas_call(
        functools.partial(kernel, SN, PN),
        out_shape=shapes,
        in_specs=[pl.BlockSpec(memory_space=pl.ANY)] * 3,
        out_specs=(pl.BlockSpec(memory_space=pl.ANY),) * 2,
        scratch_shapes=scratch,
        compiler_params=pltpu.CompilerParams(
            collective_id=0, has_side_effects=True, vmem_limit_bytes=62 * 1024 * 1024
        ),
        cost_estimate=pl.CostEstimate(
            flops=12 * flops, bytes_accessed=4 * width * (protos + 4 * rows), transcendentals=2 * rows * protos
        ),
    )(teacher_feats, student_feats, prototypes)
    return pl.pallas_call(
        finish,
        out_shape=shapes,
        in_specs=[pl.BlockSpec(memory_space=pl.ANY)] * 2,
        out_specs=(pl.BlockSpec(memory_space=pl.ANY),) * 2,
        scratch_shapes=[V((rows, width), f32), V((width // SN, protos), f32), DMA((2, 4))],
        cost_estimate=pl.CostEstimate(
            flops=0, bytes_accessed=8 * (rows * width + width // SN * protos), transcendentals=0
        ),
    )(*outs)


def solution(mesh):
    SN, PN = mesh.shape["smp"], mesh.shape["proto"]
    in_specs = (P("smp", None), P("smp", None), P(None, "proto"))
    out_specs = (P("smp", None), P("smp", "proto"))
    return jax.shard_map(
        functools.partial(local, SN, PN), mesh=mesh, in_specs=in_specs, out_specs=out_specs, check_vma=False
    )
```

```python
import functools

import jax
import jax.numpy as jnp
from jax import lax
from jax.experimental import pallas as pl
from jax.experimental.pallas import tpu as pltpu
from jax.sharding import PartitionSpec as P

ITERS = 3
TEACHER_TEMP = 0.07
STUDENT_TEMP = 0.1
LOG2E = 1.4426950408889634

YN = 4
TILE = 512
LANES = 128
MESH = pl.DeviceIdType.MESH
f32 = jnp.float32
bf16 = jnp.bfloat16


def mm(a, b):
    return jnp.dot(a, b, preferred_element_type=f32)


def mm_t(a, b):
    return lax.dot_general(a, b, (((1,), (1,)), ((), ())), preferred_element_type=f32)


def split(v):
    hi = v.astype(bf16)
    return hi, (v - hi.astype(f32)).astype(bf16)


def kernel(
    SN,
    PN,
    t_hbm,
    s_hbm,
    p_hbm,
    gf_out,
    gp_out,
    feats,
    thh,
    tl,
    shh,
    sl,
    st,
    phl,
    e,
    q,
    dh,
    dl,
    cola,
    cola_in,
    col,
    col_in,
    pscale,
    peakf,
    acc,
    mx,
    cb,
    ab,
    rowm,
    row_in,
    stat,
    stat_in,
    gfacc,
    gfs,
    gya,
    gyb,
    gfz,
    gft,
    gfz2,
    gfo,
    cr,
    xa,
    xb,
    gpo,
    load_sem,
    cs_sem,
    cr_sem,
    rs_sem,
    rr_sem,
    st_sem,
    ys_sem,
    yr_sem,
    zs_sem,
    zr_sem,
    ks_sem,
    kr_sem,
    xs_sem,
    xr_sem,
    out_sem,
):
    ZN = PN // YN
    XN = SN // 2
    rows, width = t_hbm.shape
    tiles = p_hbm.shape[1] // TILE
    per = TILE // LANES
    blocks = rows // LANES
    s = lax.axis_index("smp")
    p = lax.axis_index("proto")
    x = s // 2
    c = s % 2
    z = p // YN
    y = p % YN
    sibling = (2 * x + 1 - c, p)
    right = (2 * ((x + 1) % XN) + c, p)
    left = (2 * ((x + XN - 1) % XN) + c, p)
    y_right = (s, z * YN + (y + 1) % YN)
    y_left = (s, z * YN + (y + YN - 1) % YN)

    def far(d, n):
        return min(d, n - d)

    offsets = sorted(((dx, dc) for dx in range(XN) for dc in range(2)), key=lambda o: -far(o[0], XN))
    smp_peers = [2 * ((x + dx) % XN) + (c + dc) % 2 for dx, dc in offsets if dx or dc]
    smp_group = (s, SN, [(k, (k, p)) for k in smp_peers])
    offsets = sorted(((dz, dy) for dz in range(ZN) for dy in range(YN)), key=lambda o: -far(o[0], ZN) - far(o[1], YN))
    row_peers = [((z + dz) % ZN) * YN + (y + dy) % YN for dz, dy in offsets if dz or dy]
    row_group = (p, PN, [(k, (s, k)) for k in row_peers])
    z_peers = [(z + dz) % ZN for dz in sorted(range(1, ZN), key=lambda d: -far(d, ZN))]
    z_group = (z, ZN, [(k, (s, k * YN + y)) for k in z_peers])

    def rc(src, dst, ss, rs, dev):
        return pltpu.make_async_remote_copy(
            src_ref=src, dst_ref=dst, send_sem=ss, recv_sem=rs, device_id=dev, device_id_type=MESH
        )

    barrier = pltpu.get_barrier_semaphore()
    for _, dev in smp_group[2] + row_group[2]:
        pl.semaphore_signal(barrier, inc=1, device_id=dev, device_id_type=MESH)

    load_t = pltpu.make_async_copy(t_hbm, feats.at[0], load_sem.at[0])
    load_s = pltpu.make_async_copy(s_hbm, feats.at[1], load_sem.at[1])

    def load_p(j):
        cols = pl.ds(pl.multiple_of(j * TILE, TILE), TILE)
        return pltpu.make_async_copy(
            p_hbm.at[:, cols], q.at[j, pl.ds(0, width)], load_sem.at[2 + j]
        )

    load_t.start()
    for j in range(tiles):
        load_p(j).start()
    load_s.start()

    def group_send(src, dst, group, ssem, rsem):
        me, n, peers = group
        for k, dev in peers:
            rc(src(k), dst.at[me], ssem, rsem, dev).start()

    def group_wait(dst, group, ssem, rsem):
        me, n, peers = group
        blocks = dst.at[pl.ds(0, n - 1)]
        copy = rc(blocks, blocks, ssem, rsem, peers[0][1])
        copy.wait_recv()
        copy.wait_send()

    load_t.wait()
    hi, lo = split(feats[0] * (LOG2E / (TEACHER_TEMP / STUDENT_TEMP)))
    thh[:, 0:width] = hi
    thh[:, width : 2 * width] = hi
    tl[...] = lo

    @pl.loop(0, tiles)
    def _(j):
        load_p(j).wait()
        ph, plo = split(q[j, 0:width, :] * (1.0 / STUDENT_TEMP))
        phl[j, 0:width, :] = ph
        phl[j, width : 2 * width, :] = plo
        scores = mm(thh[...], phl[j]) + mm(tl[...], phl[j, 0:width, :])
        top = jnp.max(scores, axis=0, keepdims=True)
        ex = jnp.exp2(scores - top)
        e[j] = ex
        total = jnp.sum(ex, axis=0, keepdims=True)
        for i in range(per):
            cola[pl.ds(per * j + i, 1), :] = top[:, LANES * i : LANES * (i + 1)]
            cola[pl.ds(per * (tiles + j) + i, 1), :] = total[:, LANES * i : LANES * (i + 1)]

    pl.semaphore_wait(barrier, len(smp_peers) + len(row_peers))

    def student(first, last):
        @pl.loop(first, last)
        def _(j):
            scores = mm(shh[...], phl[j]) + mm(sl[...], phl[j, 0:width, :])
            q[j] = scores
            for r in range(blocks):
                rs = slice(LANES * r, LANES * (r + 1))
                m = mx[rs, :]
                for i in range(per):
                    m = jnp.maximum(m, scores[rs, LANES * i : LANES * (i + 1)])
                mx[rs, :] = m

    def student_start():
        load_s.wait()
        sf = feats[1]
        shi, slo = split(sf * LOG2E)
        shh[:, 0:width] = shi
        shh[:, width : 2 * width] = shi
        sl[...] = slo
        mx[...] = jnp.full(mx.shape, -jnp.inf, f32)

    def student_transpose():
        keep = width // SN
        ht, lt = split((feats[1] * (1.0 / STUDENT_TEMP)).T)
        for core in range(2):
            for chip in range(XN):
                to = (core * XN + chip) * keep
                fr = (2 * chip + core) * keep
                st[0, to : to + keep, :] = ht[fr : fr + keep, :]
                st[1, to : to + keep, :] = lt[fr : fr + keep, :]

    def to_rows(ref, reduce, out, base):
        for r in range(blocks):
            rs = slice(LANES * r, LANES * (r + 1))
            out[base + r : base + r + 1, :] = reduce(ref[rs, :].T, axis=0, keepdims=True)

    def to_columns(v, out):
        for r in range(blocks):
            rs = slice(LANES * r, LANES * (r + 1))
            out[rs, :] = jnp.broadcast_to(v[r : r + 1, :], (LANES, LANES)).T

    def student_totals():
        to_rows(mx, jnp.max, stat, 0)
        to_columns(stat[0:blocks, :], ab)
        mx[...] = jnp.zeros(mx.shape, f32)

        @pl.loop(0, tiles)
        def _(j):
            for r in range(blocks):
                rs = slice(LANES * r, LANES * (r + 1))
                m = ab[rs, :]
                a = mx[rs, :]
                for i in range(per):
                    ls = slice(LANES * i, LANES * (i + 1))
                    v = jnp.exp2(q[j, rs, ls] - m)
                    q[j, rs, ls] = v
                    a = a + v
                mx[rs, :] = a

        to_rows(mx, jnp.sum, stat, blocks)

    def row_pass(it):
        acc[...] = jnp.zeros(acc.shape, f32)

        @pl.loop(0, tiles)
        def _(j):
            ws = [pscale[pl.ds(per * j + i, 1), :] for i in range(per)]
            fs = [peakf[pl.ds(per * j + i, 1), :] for i in range(per)] if it == 0 else None
            for r in range(blocks):
                rs = slice(LANES * r, LANES * (r + 1))
                a = acc[rs, :]
                for i in range(per):
                    ls = slice(LANES * i, LANES * (i + 1))
                    v = e[j, rs, ls]
                    if it == 0:
                        v = v * fs[i]
                        e[j, rs, ls] = v
                    a = a + v * ws[i]
                acc[rs, :] = a

        to_rows(acc, jnp.sum, rowm.at[it], 0)

    def row_start(it):
        row_in[it, pl.ds(p, 1)] = rowm[it : it + 1]
        group_send(lambda k: rowm.at[it], row_in.at[it], row_group, rs_sem.at[it], rr_sem.at[it])

    def row_end(it):
        group_wait(row_in.at[it], row_group, rs_sem.at[it], rr_sem.at[it])
        mass = sum(row_in[it, k] for k in range(PN))
        to_columns(1.0 / mass, cb)

    def col_pass(it):
        @pl.loop(0, tiles)
        def _(j):
            for i in range(per):
                ls = slice(LANES * i, LANES * (i + 1))
                v = jnp.sum(e[j, :, ls] * cb[...], axis=0, keepdims=True)
                col[it, pl.ds(per * j + i, 1), :] = v

    def col_start(it):
        col_in[it, pl.ds(s, 1)] = col[it : it + 1]
        group_send(lambda k: col.at[it], col_in.at[it], smp_group, cs_sem.at[it + 1], cr_sem.at[it + 1])

    def col_end(it):
        group_wait(col_in.at[it], smp_group, cs_sem.at[it + 1], cr_sem.at[it + 1])
        pscale[...] = 1.0 / sum(col_in[it, k] for k in range(SN))

    keep = width // SN
    hk = keep // 2
    mine = pl.multiple_of(c * (width // 2), width // 2)
    other = pl.multiple_of((1 - c) * (width // 2), width // 2)
    across = pl.multiple_of(((x + 2) % XN) * keep, keep)
    ahead = pl.multiple_of(((x + 1) % XN) * keep, keep)
    behind = pl.multiple_of(((x + XN - 1) % XN) * keep, keep)
    here = pl.multiple_of(x * keep, keep)

    def core_copy(t):
        return rc(e.at[t, pl.ds(other, width // 2)], cr.at[t], ks_sem.at[t], kr_sem.at[t], sibling)

    def x_copy(t, k):
        row, dst, dev = [
            (across, xa.at[t, 0], right),
            (across + hk, xa.at[t, 1], left),
            (ahead + hk, xb.at[t, 0, pl.ds(hk, hk)], right),
            (behind, xb.at[t, 1, pl.ds(0, hk)], left),
            (ahead, xb.at[t, 0, pl.ds(0, hk)], right),
            (behind + hk, xb.at[t, 1, pl.ds(hk, hk)], left),
        ][k]
        src = cr.at[t, pl.ds(pl.multiple_of(row, 8), hk)]
        return rc(src, dst, xs_sem.at[t, k], xr_sem.at[t, k], dev)

    def out_copy(t):
        cols = pl.ds(pl.multiple_of(t * TILE, TILE), TILE)
        return pltpu.make_async_copy(gpo.at[t], gp_out.at[:, cols], out_sem.at[t])

    def gp_terms(t):
        d = dh[t]
        e[t, 0:width, :] = mm(st[0], d) + mm(st[1], d) + mm(st[0], dl[t])
        core_copy(t).start()

    def gp_core(t):
        core_copy(t).wait_recv()
        cr[t] = cr[t] + e[t, pl.ds(mine, width // 2), :]
        x_copy(t, 0).start()
        x_copy(t, 1).start()

        @pl.when(t < 2)
        def _():
            x_copy(t, 2).start()
            x_copy(t, 3).start()

    def gp_relay(t):
        x_copy(t, 0).wait_recv()
        x_copy(t, 1).wait_recv()
        a = pl.ds(pl.multiple_of(ahead, 8), hk)
        cr[t, a, :] = cr[t, a, :] + xa[t, 0]
        b = pl.ds(pl.multiple_of(behind + hk, 8), hk)
        cr[t, b, :] = cr[t, b, :] + xa[t, 1]

        @pl.when(t >= 2)
        def _():
            x_copy(t, 2).start()
            x_copy(t, 3).start()

        x_copy(t, 4).start()
        x_copy(t, 5).start()

    def gp_end(t):
        for k in range(2, 6):
            x_copy(t, k).wait_recv()
        gpo[t] = cr[t, pl.ds(here, keep), :] + xb[t, 0] + xb[t, 1]
        out_copy(t).start()
        core_copy(t).wait_send()
        for k in range(6):
            x_copy(t, k).wait_send()

    part = rows // 2
    chunk = part // YN
    hc = chunk // 2
    piece = chunk // ZN

    def chunk_at(r, d, low, size):
        return pl.ds(pl.multiple_of((r % 2) * part + ((y + d) % YN) * chunk + low, 8), size)

    def y_copy(r, k):
        d, low, dst, dev = [
            (2, 0, gya.at[r, 0], y_right),
            (2, hc, gya.at[r, 1], y_left),
            (1, hc, gyb.at[r, 0, pl.ds(hc, hc)], y_right),
            (YN - 1, 0, gyb.at[r, 1, pl.ds(0, hc)], y_left),
            (1, 0, gyb.at[r, 0, pl.ds(0, hc)], y_right),
            (YN - 1, hc, gyb.at[r, 1, pl.ds(hc, hc)], y_left),
        ][k]
        return rc(gfs.at[r // 2, chunk_at(r, d, low, hc)], dst, ys_sem.at[r, k], yr_sem.at[r, k], dev)

    def y_gather(r, k):
        d, low, size, dev = [
            (0, 0, chunk, y_right),
            (0, 0, chunk, y_left),
            (YN - 1, 0, hc, y_right),
            (1, hc, hc, y_left),
        ][k]
        src = gfo.at[chunk_at(r, d, low, size)]
        return rc(src, src, ys_sem.at[r, 6 + k], yr_sem.at[r, 6 + k], dev)

    def y_arrive(r, k):
        d, low, size = [(YN - 1, 0, chunk), (1, 0, chunk), (2, 0, hc), (2, hc, hc)][k]
        dst = gfo.at[chunk_at(r, d, low, size)]
        rc(dst, dst, ys_sem.at[r, 6 + k], yr_sem.at[r, 6 + k], y_right).wait_recv()

    def gf_a(r):
        for k in range(4):
            y_copy(r, k).start()

    def gf_b(r):
        for k in range(2):
            y_copy(r, k).wait_recv()
        a = chunk_at(r, 1, 0, hc)
        gfs[r // 2, a, :] = gfs[r // 2, a, :] + gya[r, 0]
        b = chunk_at(r, YN - 1, hc, hc)
        gfs[r // 2, b, :] = gfs[r // 2, b, :] + gya[r, 1]
        y_copy(r, 4).start()
        y_copy(r, 5).start()

    def gf_c(r):
        for k in range(2, 6):
            y_copy(r, k).wait_recv()
        for k in range(ZN):
            rs = slice(k * piece, (k + 1) * piece)
            own = gfs[r // 2, chunk_at(r, 0, k * piece, piece), :]
            gft[r, k] = own + gyb[r, 0, rs, :] + gyb[r, 1, rs, :]
        group_send(lambda k: gft.at[r, k], gfz.at[r], z_group, zs_sem.at[r], zr_sem.at[r])

    def gf_d(r):
        group_wait(gfz.at[r], z_group, zs_sem.at[r], zr_sem.at[r])
        gfz[r, pl.ds(z, 1)] = gft[r, pl.ds(z, 1)]
        if r < 2:
            targets = sum(gfz[r, k] for k in range(ZN))
            probs = sum(gfz[r + 2, k] for k in range(ZN))
            scale = cb[chunk_at(r, 0, z * piece, piece), :]
            scale = jnp.concatenate([scale] * (width // LANES), axis=1)
            gfz2[r, pl.ds(z, 1)] = (probs - scale * targets)[None]
            group_send(lambda k: gfz2.at[r, z], gfz2.at[r], z_group, zs_sem.at[4 + r], zr_sem.at[4 + r])

    def gf_e(r):
        group_wait(gfz2.at[r], z_group, zs_sem.at[4 + r], zr_sem.at[4 + r])
        for k in range(ZN):
            gfo[chunk_at(r, 0, k * piece, piece), :] = gfz2[r, k]
        y_gather(r, 0).start()
        y_gather(r, 1).start()

    def gf_f(r):
        y_arrive(r, 0)
        y_arrive(r, 1)
        y_gather(r, 2).start()
        y_gather(r, 3).start()

    def gf_copy(r):
        rs = pl.ds(r * part, part)
        return pltpu.make_async_copy(gfo.at[rs], gf_out.at[rs], out_sem.at[tiles + r])

    def gf_g(r):
        y_arrive(r, 2)
        y_arrive(r, 3)
        gf_copy(r).start()
        for k in range(6):
            y_copy(r, k).wait_send()
            y_copy(r + 2, k).wait_send()
        for k in range(4):
            y_gather(r, k).wait_send()

    def feat_terms(j, which, rs):
        gfacc[which, rs, :] += mm_t(dh[j, rs, :], phl[j])
        gfacc[which, rs, 0:width] += mm_t(dl[j, rs, :], phl[j, 0:width, :])

    everything = slice(0, rows)
    halves = [slice(0, part), slice(part, rows)]

    def probs_terms(first, last):
        @pl.loop(first, last)
        def _(j):
            hi, lo = split(q[j])
            dh[j] = hi
            dl[j] = lo
            feat_terms(j, 1, everything)

    def probs_sum():
        for k in range(width // LANES):
            ls = slice(LANES * k, LANES * (k + 1))
            us = slice(width + LANES * k, width + LANES * (k + 1))
            gfs[1, :, ls] = (gfacc[1, :, ls] + gfacc[1, :, us]) * ab[...]
        gf_a(2)
        gf_a(3)

    def mass_terms(h, first, last):
        @pl.loop(first, last)
        def _(j):
            if h == 0:
                for k in range(per):
                    ls = slice(LANES * k, LANES * (k + 1))
                    hi, lo = split(e[j, :, ls] * pscale[pl.ds(per * j + k, 1), :])
                    dh[j, :, ls] = hi
                    dl[j, :, ls] = lo
            feat_terms(j, 0, halves[h])

    def mass_sum(h):
        rs = halves[h]
        gfs[0, rs, :] = gfacc[0, rs, 0:width] + gfacc[0, rs, width : 2 * width]
        gf_a(h)

    half = per * tiles
    cola_in[pl.ds(s, 1)] = cola[...][None]
    group_send(lambda k: cola, cola_in, smp_group, cs_sem.at[0], cr_sem.at[0])
    student_start()
    student(0, 5)
    gfacc[...] = jnp.zeros(gfacc.shape, f32)
    group_wait(cola_in, smp_group, cs_sem.at[0], cr_sem.at[0])
    tops = [cola_in[k, 0:half, :] for k in range(SN)]
    top = functools.reduce(jnp.maximum, tops)
    pscale[...] = 1.0 / sum(cola_in[k, half : 2 * half, :] * jnp.exp2(tops[k] - top) for k in range(SN))
    peakf[...] = jnp.exp2(cola[0:half, :] - top)

    row_pass(0)
    row_start(0)
    student(5, tiles)
    student_totals()
    row_end(0)
    col_pass(0)
    col_start(0)
    stat_in[pl.ds(p, 1)] = stat[...][None]
    group_send(lambda k: stat, stat_in, row_group, st_sem.at[0], st_sem.at[1])
    probs_terms(0, 4)
    col_end(0)

    row_pass(1)
    row_start(1)
    probs_terms(4, tiles)
    group_wait(stat_in, row_group, st_sem.at[0], st_sem.at[1])
    tops = [stat_in[k, 0:blocks, :] for k in range(PN)]
    top = functools.reduce(jnp.maximum, tops)
    total = sum(stat_in[k, blocks : 2 * blocks, :] * jnp.exp2(tops[k] - top) for k in range(PN))
    to_columns(jnp.exp2(stat[0:blocks, :] - top) / total, ab)
    row_end(1)
    col_pass(1)
    col_start(1)
    probs_sum()
    student_transpose()
    col_end(1)

    row_pass(2)
    row_start(2)
    gf_b(2)
    gf_b(3)
    mass_terms(0, 0, tiles)
    mass_sum(0)
    mass_terms(1, 0, 2)
    row_end(2)

    lag_core, lag_relay, lag_end = 2, 6, 10
    at = {
        2: [(gf_c, 2), (gf_c, 3)],
        3: [(gf_c, 0)],
        4: [(gf_b, 1)],
        7: [(gf_d, 2), (gf_d, 3)],
        8: [(gf_c, 1)],
        9: [(gf_d, 0)],
        11: [(gf_d, 1)],
        12: [(gf_e, 0)],
        13: [(gf_e, 1)],
        14: [(gf_f, 0)],
        15: [(gf_f, 1)],
        16: [(gf_g, 0)],
        17: [(gf_g, 1)],
    }

    def dlogits(i):
        for k in range(per):
            ls = slice(LANES * k, LANES * (k + 1))
            w = pscale[pl.ds(per * i + k, 1), :]
            d = q[i, :, ls] * ab[...] - (cb[...] * e[i, :, ls]) * w
            dhi, dlo = split(d)
            dh[i, :, ls] = dhi
            dl[i, :, ls] = dlo

    @pl.loop(0, 2)
    def _(i):
        dlogits(i)
        gp_terms(i)

    mass_terms(1, 2, 5)
    gf_b(0)
    gp_core(0)
    mass_terms(1, 5, tiles)
    mass_sum(1)
    gp_core(1)

    @pl.loop(2, tiles + lag_end)
    def _(i):
        @pl.when(i < tiles)
        def _():
            dlogits(i)
            gp_terms(i)

        @pl.when((i >= 2 + lag_core) & (i < tiles + lag_core))
        def _():
            gp_core(i - lag_core)

        @pl.when((i >= lag_relay) & (i < tiles + lag_relay))
        def _():
            gp_relay(i - lag_relay)

        for when, todo in at.items():

            @pl.when(i == when)
            def _(todo=todo):
                for f, h in todo:
                    f(h)

        @pl.when(i >= lag_end)
        def _():
            gp_end(i - lag_end)

    for t in range(tiles):
        out_copy(t).wait()
    for h in range(2):
        gf_copy(h).wait()


def finish(gf_in, gp_in, gf_out, gp_out, gf_mid, gp_mid, sem):
    copies = []
    for k, (src, mid, dst) in enumerate(((gf_in, gf_mid, gf_out), (gp_in, gp_mid, gp_out))):
        n = src.shape[0] // 2
        for h in range(2):
            rs = pl.ds(h * n, n)
            first = pltpu.make_async_copy(src.at[rs], mid.at[rs], sem.at[0, 2 * k + h])
            second = pltpu.make_async_copy(mid.at[rs], dst.at[rs], sem.at[1, 2 * k + h])
            first.start()
            copies.append((first, second))
    for first, second in copies:
        first.wait()
        second.start()
    for first, second in copies:
        second.wait()


def local(SN, PN, teacher_feats, student_feats, prototypes):
    rows, width = teacher_feats.shape
    protos = prototypes.shape[1]
    tiles = protos // TILE
    half = protos // LANES
    blocks = rows // LANES
    ZN = PN // YN
    chunk = rows // 2 // YN
    piece = chunk // ZN
    V = pltpu.VMEM
    DMA = pltpu.SemaphoreType.DMA
    scratch = [
        V((2, rows, width), f32),
        V((rows, 2 * width), bf16),
        V((rows, width), bf16),
        V((rows, 2 * width), bf16),
        V((rows, width), bf16),
        V((2, width, rows), bf16),
        V((tiles, 2 * width, TILE), bf16),
        V((tiles, rows, TILE), f32),
        V((tiles, rows, TILE), f32),
        V((tiles, rows, TILE), bf16),
        V((tiles, rows, TILE), bf16),
        V((2 * half, LANES), f32),
        V((SN, 2 * half, LANES), f32),
        V((ITERS - 1, half, LANES), f32),
        V((ITERS - 1, SN, half, LANES), f32),
        V((half, LANES), f32),
        V((half, LANES), f32),
        V((rows, LANES), f32),
        V((rows, LANES), f32),
        V((rows, LANES), f32),
        V((rows, LANES), f32),
        V((ITERS, blocks, LANES), f32),
        V((ITERS, PN, blocks, LANES), f32),
        V((2 * blocks, LANES), f32),
        V((PN, 2 * blocks, LANES), f32),
        V((2, rows, 2 * width), f32),
        V((2, rows, width), f32),
        V((4, 2, chunk // 2, width), f32),
        V((4, 2, chunk, width), f32),
        V((4, ZN, piece, width), f32),
        V((4, ZN, piece, width), f32),
        V((2, ZN, piece, width), f32),
        V((rows, width), f32),
        V((tiles, width // 2, TILE), f32),
        V((tiles, 2, width // SN // 2, TILE), f32),
        V((tiles, 2, width // SN, TILE), f32),
        V((tiles, width // SN, TILE), f32),
        DMA((2 + tiles,)),
        DMA((ITERS,)),
        DMA((ITERS,)),
        DMA((ITERS,)),
        DMA((ITERS,)),
        DMA((2,)),
        DMA((4, 10)),
        DMA((4, 10)),
        DMA((6,)),
        DMA((6,)),
        DMA((tiles,)),
        DMA((tiles,)),
        DMA((tiles, 6)),
        DMA((tiles, 6)),
        DMA((tiles + 2,)),
    ]
    flops = 2 * rows * width * protos
    shapes = (
        jax.ShapeDtypeStruct((rows, width), f32),
        jax.ShapeDtypeStruct((width // SN, protos), f32),
    )
    outs = pl.pallas_call(
        functools.partial(kernel, SN, PN),
        out_shape=shapes,
        in_specs=[pl.BlockSpec(memory_space=pl.ANY)] * 3,
        out_specs=(pl.BlockSpec(memory_space=pl.ANY),) * 2,
        scratch_shapes=scratch,
        compiler_params=pltpu.CompilerParams(
            collective_id=0, has_side_effects=True, vmem_limit_bytes=62 * 1024 * 1024
        ),
        cost_estimate=pl.CostEstimate(
            flops=12 * flops, bytes_accessed=4 * width * (protos + 4 * rows), transcendentals=2 * rows * protos
        ),
    )(teacher_feats, student_feats, prototypes)
    return pl.pallas_call(
        finish,
        out_shape=shapes,
        in_specs=[pl.BlockSpec(memory_space=pl.ANY)] * 2,
        out_specs=(pl.BlockSpec(memory_space=pl.ANY),) * 2,
        scratch_shapes=[V((rows, width), f32), V((width // SN, protos), f32), DMA((2, 4))],
        cost_estimate=pl.CostEstimate(
            flops=0, bytes_accessed=8 * (rows * width + width // SN * protos), transcendentals=0
        ),
    )(*outs)


def solution(mesh):
    SN, PN = mesh.shape["smp"], mesh.shape["proto"]
    in_specs = (P("smp", None), P("smp", None), P(None, "proto"))
    out_specs = (P("smp", None), P("smp", "proto"))
    return jax.shard_map(
        functools.partial(local, SN, PN), mesh=mesh, in_specs=in_specs, out_specs=out_specs, check_vma=False
    )
```

```python
import functools

import jax
import jax.numpy as jnp
from jax import lax
from jax.experimental import pallas as pl
from jax.experimental.pallas import tpu as pltpu
from jax.sharding import PartitionSpec as P

ITERS = 3
TEACHER_TEMP = 0.07
STUDENT_TEMP = 0.1
LOG2E = 1.4426950408889634

YN = 4
TILE = 512
LANES = 128
MESH = pl.DeviceIdType.MESH
f32 = jnp.float32
bf16 = jnp.bfloat16


def mm(a, b):
    return jnp.dot(a, b, preferred_element_type=f32)


def mm_t(a, b):
    return lax.dot_general(a, b, (((1,), (1,)), ((), ())), preferred_element_type=f32)


def split(v):
    hi = v.astype(bf16)
    return hi, (v - hi.astype(f32)).astype(bf16)


def kernel(
    SN,
    PN,
    t_hbm,
    s_hbm,
    p_hbm,
    gf_out,
    gp_out,
    feats,
    thh,
    tl,
    shh,
    sl,
    st,
    phl,
    e,
    q,
    dh,
    dl,
    cola,
    cola_in,
    col,
    col_in,
    pscale,
    peakf,
    acc,
    mx,
    cb,
    ab,
    rowm,
    row_in,
    stat,
    stat_in,
    gfacc,
    gfs,
    gya,
    gyb,
    gfz,
    gft,
    gfz2,
    gfo,
    cr,
    xa,
    xb,
    load_sem,
    cs_sem,
    cr_sem,
    rs_sem,
    rr_sem,
    st_sem,
    ys_sem,
    yr_sem,
    zs_sem,
    zr_sem,
    ks_sem,
    kr_sem,
    xs_sem,
    xr_sem,
):
    ZN = PN // YN
    XN = SN // 2
    rows, width = t_hbm.shape
    tiles = p_hbm.shape[1] // TILE
    per = TILE // LANES
    blocks = rows // LANES
    s = lax.axis_index("smp")
    p = lax.axis_index("proto")
    x = s // 2
    c = s % 2
    z = p // YN
    y = p % YN
    sibling = (2 * x + 1 - c, p)
    right = (2 * ((x + 1) % XN) + c, p)
    left = (2 * ((x + XN - 1) % XN) + c, p)
    y_right = (s, z * YN + (y + 1) % YN)
    y_left = (s, z * YN + (y + YN - 1) % YN)

    def far(d, n):
        return min(d, n - d)

    offsets = sorted(((dx, dc) for dx in range(XN) for dc in range(2)), key=lambda o: -far(o[0], XN))
    smp_peers = [2 * ((x + dx) % XN) + (c + dc) % 2 for dx, dc in offsets if dx or dc]
    smp_group = (s, SN, [(k, (k, p)) for k in smp_peers])
    offsets = sorted(((dz, dy) for dz in range(ZN) for dy in range(YN)), key=lambda o: -far(o[0], ZN) - far(o[1], YN))
    row_peers = [((z + dz) % ZN) * YN + (y + dy) % YN for dz, dy in offsets if dz or dy]
    row_group = (p, PN, [(k, (s, k)) for k in row_peers])
    z_peers = [(z + dz) % ZN for dz in sorted(range(1, ZN), key=lambda d: -far(d, ZN))]
    z_group = (z, ZN, [(k, (s, k * YN + y)) for k in z_peers])

    def rc(src, dst, ss, rs, dev):
        return pltpu.make_async_remote_copy(
            src_ref=src, dst_ref=dst, send_sem=ss, recv_sem=rs, device_id=dev, device_id_type=MESH
        )

    barrier = pltpu.get_barrier_semaphore()
    for _, dev in smp_group[2] + row_group[2]:
        pl.semaphore_signal(barrier, inc=1, device_id=dev, device_id_type=MESH)

    load_t = pltpu.make_async_copy(t_hbm, feats.at[0], load_sem.at[0])
    load_s = pltpu.make_async_copy(s_hbm, feats.at[1], load_sem.at[1])

    def load_p(j):
        cols = pl.ds(pl.multiple_of(j * TILE, TILE), TILE)
        return pltpu.make_async_copy(
            p_hbm.at[:, cols], q.at[j, pl.ds(0, width)], load_sem.at[2 + j]
        )

    load_t.start()
    for j in range(tiles):
        load_p(j).start()
    load_s.start()

    def group_send(src, dst, group, ssem, rsem):
        me, n, peers = group
        for k, dev in peers:
            rc(src(k), dst.at[me], ssem, rsem, dev).start()

    def group_wait(dst, group, ssem, rsem):
        me, n, peers = group
        blocks = dst.at[pl.ds(0, n - 1)]
        copy = rc(blocks, blocks, ssem, rsem, peers[0][1])
        copy.wait_recv()
        copy.wait_send()

    load_t.wait()
    hi, lo = split(feats[0] * (LOG2E / (TEACHER_TEMP / STUDENT_TEMP)))
    thh[:, 0:width] = hi
    thh[:, width : 2 * width] = hi
    tl[...] = lo

    @pl.loop(0, tiles)
    def _(j):
        load_p(j).wait()
        ph, plo = split(q[j, 0:width, :] * (1.0 / STUDENT_TEMP))
        phl[j, 0:width, :] = ph
        phl[j, width : 2 * width, :] = plo
        scores = mm(thh[...], phl[j]) + mm(tl[...], phl[j, 0:width, :])
        top = jnp.max(scores, axis=0, keepdims=True)
        ex = jnp.exp2(scores - top)
        e[j] = ex
        total = jnp.sum(ex, axis=0, keepdims=True)
        for i in range(per):
            cola[pl.ds(per * j + i, 1), :] = top[:, LANES * i : LANES * (i + 1)]
            cola[pl.ds(per * (tiles + j) + i, 1), :] = total[:, LANES * i : LANES * (i + 1)]

    pl.semaphore_wait(barrier, len(smp_peers) + len(row_peers))

    def student(first, last):
        @pl.loop(first, last)
        def _(j):
            scores = mm(shh[...], phl[j]) + mm(sl[...], phl[j, 0:width, :])
            q[j] = scores
            for r in range(blocks):
                rs = slice(LANES * r, LANES * (r + 1))
                m = mx[rs, :]
                for i in range(per):
                    m = jnp.maximum(m, scores[rs, LANES * i : LANES * (i + 1)])
                mx[rs, :] = m

    def student_start():
        load_s.wait()
        sf = feats[1]
        shi, slo = split(sf * LOG2E)
        shh[:, 0:width] = shi
        shh[:, width : 2 * width] = shi
        sl[...] = slo
        mx[...] = jnp.full(mx.shape, -jnp.inf, f32)

    def student_transpose():
        keep = width // SN
        ht, lt = split((feats[1] * (1.0 / STUDENT_TEMP)).T)
        for core in range(2):
            for chip in range(XN):
                to = (core * XN + chip) * keep
                fr = (2 * chip + core) * keep
                st[0, to : to + keep, :] = ht[fr : fr + keep, :]
                st[1, to : to + keep, :] = lt[fr : fr + keep, :]

    def to_rows(ref, reduce, out, base):
        for r in range(blocks):
            rs = slice(LANES * r, LANES * (r + 1))
            out[base + r : base + r + 1, :] = reduce(ref[rs, :].T, axis=0, keepdims=True)

    def to_columns(v, out):
        for r in range(blocks):
            rs = slice(LANES * r, LANES * (r + 1))
            out[rs, :] = jnp.broadcast_to(v[r : r + 1, :], (LANES, LANES)).T

    def student_totals():
        to_rows(mx, jnp.max, stat, 0)
        to_columns(stat[0:blocks, :], ab)
        mx[...] = jnp.zeros(mx.shape, f32)

        @pl.loop(0, tiles)
        def _(j):
            for r in range(blocks):
                rs = slice(LANES * r, LANES * (r + 1))
                m = ab[rs, :]
                a = mx[rs, :]
                for i in range(per):
                    ls = slice(LANES * i, LANES * (i + 1))
                    v = jnp.exp2(q[j, rs, ls] - m)
                    q[j, rs, ls] = v
                    a = a + v
                mx[rs, :] = a

        to_rows(mx, jnp.sum, stat, blocks)

    def row_pass(it):
        acc[...] = jnp.zeros(acc.shape, f32)

        @pl.loop(0, tiles)
        def _(j):
            ws = [pscale[pl.ds(per * j + i, 1), :] for i in range(per)]
            fs = [peakf[pl.ds(per * j + i, 1), :] for i in range(per)] if it == 0 else None
            for r in range(blocks):
                rs = slice(LANES * r, LANES * (r + 1))
                a = acc[rs, :]
                for i in range(per):
                    ls = slice(LANES * i, LANES * (i + 1))
                    v = e[j, rs, ls]
                    if it == 0:
                        v = v * fs[i]
                        e[j, rs, ls] = v
                    a = a + v * ws[i]
                acc[rs, :] = a

        to_rows(acc, jnp.sum, rowm.at[it], 0)

    def row_start(it):
        row_in[it, pl.ds(p, 1)] = rowm[it : it + 1]
        group_send(lambda k: rowm.at[it], row_in.at[it], row_group, rs_sem.at[it], rr_sem.at[it])

    def row_end(it):
        group_wait(row_in.at[it], row_group, rs_sem.at[it], rr_sem.at[it])
        mass = sum(row_in[it, k] for k in range(PN))
        to_columns(1.0 / mass, cb)

    def col_pass(it):
        @pl.loop(0, tiles)
        def _(j):
            for i in range(per):
                ls = slice(LANES * i, LANES * (i + 1))
                v = jnp.sum(e[j, :, ls] * cb[...], axis=0, keepdims=True)
                col[it, pl.ds(per * j + i, 1), :] = v

    def col_start(it):
        col_in[it, pl.ds(s, 1)] = col[it : it + 1]
        group_send(lambda k: col.at[it], col_in.at[it], smp_group, cs_sem.at[it + 1], cr_sem.at[it + 1])

    def col_end(it):
        group_wait(col_in.at[it], smp_group, cs_sem.at[it + 1], cr_sem.at[it + 1])
        pscale[...] = 1.0 / sum(col_in[it, k] for k in range(SN))

    keep = width // SN
    hk = keep // 2
    mine = pl.multiple_of(c * (width // 2), width // 2)
    other = pl.multiple_of((1 - c) * (width // 2), width // 2)
    across = pl.multiple_of(((x + 2) % XN) * keep, keep)
    ahead = pl.multiple_of(((x + 1) % XN) * keep, keep)
    behind = pl.multiple_of(((x + XN - 1) % XN) * keep, keep)
    here = pl.multiple_of(x * keep, keep)

    def core_copy(t):
        return rc(e.at[t, pl.ds(other, width // 2)], cr.at[t], ks_sem.at[t], kr_sem.at[t], sibling)

    def x_copy(t, k):
        row, dst, dev = [
            (across, xa.at[t, 0], right),
            (across + hk, xa.at[t, 1], left),
            (ahead + hk, xb.at[t, 0, pl.ds(hk, hk)], right),
            (behind, xb.at[t, 1, pl.ds(0, hk)], left),
            (ahead, xb.at[t, 0, pl.ds(0, hk)], right),
            (behind + hk, xb.at[t, 1, pl.ds(hk, hk)], left),
        ][k]
        src = cr.at[t, pl.ds(pl.multiple_of(row, 8), hk)]
        return rc(src, dst, xs_sem.at[t, k], xr_sem.at[t, k], dev)

    def gp_terms(t):
        d = dh[t]
        e[t, 0:width, :] = mm(st[0], d) + mm(st[1], d) + mm(st[0], dl[t])
        core_copy(t).start()

    def gp_core(t):
        core_copy(t).wait_recv()
        cr[t] = cr[t] + e[t, pl.ds(mine, width // 2), :]
        x_copy(t, 0).start()
        x_copy(t, 1).start()

        @pl.when(t < 2)
        def _():
            x_copy(t, 2).start()
            x_copy(t, 3).start()

    def gp_relay(t):
        x_copy(t, 0).wait_recv()
        x_copy(t, 1).wait_recv()
        a = pl.ds(pl.multiple_of(ahead, 8), hk)
        cr[t, a, :] = cr[t, a, :] + xa[t, 0]
        b = pl.ds(pl.multiple_of(behind + hk, 8), hk)
        cr[t, b, :] = cr[t, b, :] + xa[t, 1]

        @pl.when(t >= 2)
        def _():
            x_copy(t, 2).start()
            x_copy(t, 3).start()

        x_copy(t, 4).start()
        x_copy(t, 5).start()

    def gp_end(t):
        for k in range(2, 6):
            x_copy(t, k).wait_recv()
        cols = pl.ds(pl.multiple_of(t * TILE, TILE), TILE)
        gp_out[:, cols] = cr[t, pl.ds(here, keep), :] + xb[t, 0] + xb[t, 1]
        core_copy(t).wait_send()
        for k in range(6):
            x_copy(t, k).wait_send()

    part = rows // 2
    chunk = part // YN
    hc = chunk // 2
    piece = chunk // ZN

    def chunk_at(r, d, low, size):
        return pl.ds(pl.multiple_of((r % 2) * part + ((y + d) % YN) * chunk + low, 8), size)

    def y_copy(r, k):
        d, low, dst, dev = [
            (2, 0, gya.at[r, 0], y_right),
            (2, hc, gya.at[r, 1], y_left),
            (1, hc, gyb.at[r, 0, pl.ds(hc, hc)], y_right),
            (YN - 1, 0, gyb.at[r, 1, pl.ds(0, hc)], y_left),
            (1, 0, gyb.at[r, 0, pl.ds(0, hc)], y_right),
            (YN - 1, hc, gyb.at[r, 1, pl.ds(hc, hc)], y_left),
        ][k]
        return rc(gfs.at[r // 2, chunk_at(r, d, low, hc)], dst, ys_sem.at[r, k], yr_sem.at[r, k], dev)

    def y_gather(r, k):
        d, low, size, dev = [
            (0, 0, chunk, y_right),
            (0, 0, chunk, y_left),
            (YN - 1, 0, hc, y_right),
            (1, hc, hc, y_left),
        ][k]
        src = gfo.at[chunk_at(r, d, low, size)]
        return rc(src, src, ys_sem.at[r, 6 + k], yr_sem.at[r, 6 + k], dev)

    def y_arrive(r, k):
        d, low, size = [(YN - 1, 0, chunk), (1, 0, chunk), (2, 0, hc), (2, hc, hc)][k]
        dst = gfo.at[chunk_at(r, d, low, size)]
        rc(dst, dst, ys_sem.at[r, 6 + k], yr_sem.at[r, 6 + k], y_right).wait_recv()

    def gf_a(r):
        for k in range(4):
            y_copy(r, k).start()

    def gf_b(r):
        for k in range(2):
            y_copy(r, k).wait_recv()
        a = chunk_at(r, 1, 0, hc)
        gfs[r // 2, a, :] = gfs[r // 2, a, :] + gya[r, 0]
        b = chunk_at(r, YN - 1, hc, hc)
        gfs[r // 2, b, :] = gfs[r // 2, b, :] + gya[r, 1]
        y_copy(r, 4).start()
        y_copy(r, 5).start()

    def gf_c(r):
        for k in range(2, 6):
            y_copy(r, k).wait_recv()
        for k in range(ZN):
            rs = slice(k * piece, (k + 1) * piece)
            own = gfs[r // 2, chunk_at(r, 0, k * piece, piece), :]
            gft[r, k] = own + gyb[r, 0, rs, :] + gyb[r, 1, rs, :]
        group_send(lambda k: gft.at[r, k], gfz.at[r], z_group, zs_sem.at[r], zr_sem.at[r])

    def gf_d(r):
        group_wait(gfz.at[r], z_group, zs_sem.at[r], zr_sem.at[r])
        gfz[r, pl.ds(z, 1)] = gft[r, pl.ds(z, 1)]
        if r < 2:
            targets = sum(gfz[r, k] for k in range(ZN))
            probs = sum(gfz[r + 2, k] for k in range(ZN))
            scale = cb[chunk_at(r, 0, z * piece, piece), :]
            scale = jnp.concatenate([scale] * (width // LANES), axis=1)
            gfz2[r, pl.ds(z, 1)] = (probs - scale * targets)[None]
            group_send(lambda k: gfz2.at[r, z], gfz2.at[r], z_group, zs_sem.at[4 + r], zr_sem.at[4 + r])

    def gf_e(r):
        group_wait(gfz2.at[r], z_group, zs_sem.at[4 + r], zr_sem.at[4 + r])
        for k in range(ZN):
            gfo[chunk_at(r, 0, k * piece, piece), :] = gfz2[r, k]
        y_gather(r, 0).start()
        y_gather(r, 1).start()

    def gf_f(r):
        y_arrive(r, 0)
        y_arrive(r, 1)
        y_gather(r, 2).start()
        y_gather(r, 3).start()

    def gf_g(r):
        y_arrive(r, 2)
        y_arrive(r, 3)
        rs = pl.ds(r * part, part)
        gf_out[rs, :] = gfo[rs, :]
        for k in range(6):
            y_copy(r, k).wait_send()
            y_copy(r + 2, k).wait_send()
        for k in range(4):
            y_gather(r, k).wait_send()

    def feat_terms(j, which, rs):
        gfacc[which, rs, :] += mm_t(dh[j, rs, :], phl[j])
        gfacc[which, rs, 0:width] += mm_t(dl[j, rs, :], phl[j, 0:width, :])

    everything = slice(0, rows)
    halves = [slice(0, part), slice(part, rows)]

    def probs_terms(first, last):
        @pl.loop(first, last)
        def _(j):
            hi, lo = split(q[j])
            dh[j] = hi
            dl[j] = lo
            feat_terms(j, 1, everything)

    def probs_sum():
        for k in range(width // LANES):
            ls = slice(LANES * k, LANES * (k + 1))
            us = slice(width + LANES * k, width + LANES * (k + 1))
            gfs[1, :, ls] = (gfacc[1, :, ls] + gfacc[1, :, us]) * ab[...]
        gf_a(2)
        gf_a(3)

    def mass_terms(h, first, last):
        @pl.loop(first, last)
        def _(j):
            if h == 0:
                for k in range(per):
                    ls = slice(LANES * k, LANES * (k + 1))
                    hi, lo = split(e[j, :, ls] * pscale[pl.ds(per * j + k, 1), :])
                    dh[j, :, ls] = hi
                    dl[j, :, ls] = lo
            feat_terms(j, 0, everything)

    def mass_sum(h):
        rs = halves[h]
        gfs[0, rs, :] = gfacc[0, rs, 0:width] + gfacc[0, rs, width : 2 * width]
        gf_a(h)

    half = per * tiles
    cola_in[pl.ds(s, 1)] = cola[...][None]
    group_send(lambda k: cola, cola_in, smp_group, cs_sem.at[0], cr_sem.at[0])
    student_start()
    student(0, 5)
    gfacc[...] = jnp.zeros(gfacc.shape, f32)
    group_wait(cola_in, smp_group, cs_sem.at[0], cr_sem.at[0])
    tops = [cola_in[k, 0:half, :] for k in range(SN)]
    top = functools.reduce(jnp.maximum, tops)
    pscale[...] = 1.0 / sum(cola_in[k, half : 2 * half, :] * jnp.exp2(tops[k] - top) for k in range(SN))
    peakf[...] = jnp.exp2(cola[0:half, :] - top)

    row_pass(0)
    row_start(0)
    student(5, tiles)
    student_totals()
    row_end(0)
    col_pass(0)
    col_start(0)
    stat_in[pl.ds(p, 1)] = stat[...][None]
    group_send(lambda k: stat, stat_in, row_group, st_sem.at[0], st_sem.at[1])
    probs_terms(0, 4)
    col_end(0)

    row_pass(1)
    row_start(1)
    probs_terms(4, tiles)
    group_wait(stat_in, row_group, st_sem.at[0], st_sem.at[1])
    tops = [stat_in[k, 0:blocks, :] for k in range(PN)]
    top = functools.reduce(jnp.maximum, tops)
    total = sum(stat_in[k, blocks : 2 * blocks, :] * jnp.exp2(tops[k] - top) for k in range(PN))
    to_columns(jnp.exp2(stat[0:blocks, :] - top) / total, ab)
    row_end(1)
    col_pass(1)
    col_start(1)
    probs_sum()
    student_transpose()
    col_end(1)

    row_pass(2)
    row_start(2)
    gf_b(2)
    gf_b(3)
    mass_terms(0, 0, tiles)
    mass_sum(0)
    mass_sum(1)
    row_end(2)

    lag_core, lag_relay, lag_end = 2, 6, 10
    at = {
        2: [(gf_c, 2), (gf_c, 3)],
        4: [(gf_c, 0)],
        3: [(gf_b, 1)],
        6: [(gf_d, 2), (gf_d, 3)],
        5: [(gf_c, 1)],
        9: [(gf_d, 0)],
        11: [(gf_d, 1)],
        12: [(gf_e, 0)],
        13: [(gf_e, 1)],
        14: [(gf_f, 0)],
        15: [(gf_f, 1)],
        16: [(gf_g, 0)],
        17: [(gf_g, 1)],
    }

    def dlogits(i):
        for k in range(per):
            ls = slice(LANES * k, LANES * (k + 1))
            w = pscale[pl.ds(per * i + k, 1), :]
            d = q[i, :, ls] * ab[...] - (cb[...] * e[i, :, ls]) * w
            dhi, dlo = split(d)
            dh[i, :, ls] = dhi
            dl[i, :, ls] = dlo

    @pl.loop(0, 2)
    def _(i):
        dlogits(i)
        gp_terms(i)

    gf_b(0)

    @pl.loop(2, tiles + lag_end)
    def _(i):
        @pl.when(i < tiles)
        def _():
            dlogits(i)
            gp_terms(i)

        @pl.when((i >= lag_core) & (i < tiles + lag_core))
        def _():
            gp_core(i - lag_core)

        @pl.when((i >= lag_relay) & (i < tiles + lag_relay))
        def _():
            gp_relay(i - lag_relay)

        for when, todo in at.items():

            @pl.when(i == when)
            def _(todo=todo):
                for f, h in todo:
                    f(h)

        @pl.when(i >= lag_end)
        def _():
            gp_end(i - lag_end)


def finish(gf_in, gp_in, gf_out, gp_out, sem):
    copies = []
    for k, (src, dst) in enumerate(((gf_in, gf_out), (gp_in, gp_out))):
        n = src.shape[0] // 2
        for h in range(2):
            rs = pl.ds(h * n, n)
            copies.append(pltpu.make_async_copy(src.at[rs], dst.at[rs], sem.at[2 * k + h]))
    for copy in copies:
        copy.start()
    for copy in copies:
        copy.wait()


def local(SN, PN, teacher_feats, student_feats, prototypes):
    rows, width = teacher_feats.shape
    protos = prototypes.shape[1]
    tiles = protos // TILE
    half = protos // LANES
    blocks = rows // LANES
    ZN = PN // YN
    chunk = rows // 2 // YN
    piece = chunk // ZN
    V = pltpu.VMEM
    DMA = pltpu.SemaphoreType.DMA
    scratch = [
        V((2, rows, width), f32),
        V((rows, 2 * width), bf16),
        V((rows, width), bf16),
        V((rows, 2 * width), bf16),
        V((rows, width), bf16),
        V((2, width, rows), bf16),
        V((tiles, 2 * width, TILE), bf16),
        V((tiles, rows, TILE), f32),
        V((tiles, rows, TILE), f32),
        V((tiles, rows, TILE), bf16),
        V((tiles, rows, TILE), bf16),
        V((2 * half, LANES), f32),
        V((SN, 2 * half, LANES), f32),
        V((ITERS - 1, half, LANES), f32),
        V((ITERS - 1, SN, half, LANES), f32),
        V((half, LANES), f32),
        V((half, LANES), f32),
        V((rows, LANES), f32),
        V((rows, LANES), f32),
        V((rows, LANES), f32),
        V((rows, LANES), f32),
        V((ITERS, blocks, LANES), f32),
        V((ITERS, PN, blocks, LANES), f32),
        V((2 * blocks, LANES), f32),
        V((PN, 2 * blocks, LANES), f32),
        V((2, rows, 2 * width), f32),
        V((2, rows, width), f32),
        V((4, 2, chunk // 2, width), f32),
        V((4, 2, chunk, width), f32),
        V((4, ZN, piece, width), f32),
        V((4, ZN, piece, width), f32),
        V((2, ZN, piece, width), f32),
        V((rows, width), f32),
        V((tiles, width // 2, TILE), f32),
        V((tiles, 2, width // SN // 2, TILE), f32),
        V((tiles, 2, width // SN, TILE), f32),
        DMA((2 + tiles,)),
        DMA((ITERS,)),
        DMA((ITERS,)),
        DMA((ITERS,)),
        DMA((ITERS,)),
        DMA((2,)),
        DMA((4, 10)),
        DMA((4, 10)),
        DMA((6,)),
        DMA((6,)),
        DMA((tiles,)),
        DMA((tiles,)),
        DMA((tiles, 6)),
        DMA((tiles, 6)),
    ]
    flops = 2 * rows * width * protos
    shapes = (
        jax.ShapeDtypeStruct((rows, width), f32),
        jax.ShapeDtypeStruct((width // SN, protos), f32),
    )
    outs = pl.pallas_call(
        functools.partial(kernel, SN, PN),
        out_shape=tuple(V(o.shape, o.dtype) for o in shapes),
        in_specs=[pl.BlockSpec(memory_space=pl.ANY)] * 3,
        out_specs=(pl.BlockSpec(memory_space=pltpu.VMEM),) * 2,
        scratch_shapes=scratch,
        compiler_params=pltpu.CompilerParams(
            collective_id=0, has_side_effects=True, vmem_limit_bytes=60 * 1024 * 1024
        ),
        cost_estimate=pl.CostEstimate(
            flops=12 * flops, bytes_accessed=4 * width * (protos + 4 * rows), transcendentals=2 * rows * protos
        ),
    )(teacher_feats, student_feats, prototypes)
    return pl.pallas_call(
        finish,
        out_shape=shapes,
        in_specs=[pl.BlockSpec(memory_space=pltpu.VMEM)] * 2,
        out_specs=(pl.BlockSpec(memory_space=pl.ANY),) * 2,
        scratch_shapes=[DMA((4,))],
        compiler_params=pltpu.CompilerParams(vmem_limit_bytes=4 * 1024 * 1024),
        cost_estimate=pl.CostEstimate(
            flops=0, bytes_accessed=8 * (rows * width + width // SN * protos), transcendentals=0
        ),
    )(*outs)


def solution(mesh):
    SN, PN = mesh.shape["smp"], mesh.shape["proto"]
    in_specs = (P("smp", None), P("smp", None), P(None, "proto"))
    out_specs = (P("smp", None), P("smp", "proto"))
    return jax.shard_map(
        functools.partial(local, SN, PN), mesh=mesh, in_specs=in_specs, out_specs=out_specs, check_vma=False
    )
```

```python
import functools

import jax
import jax.numpy as jnp
from jax import lax
from jax.experimental import pallas as pl
from jax.experimental.pallas import tpu as pltpu
from jax.sharding import PartitionSpec as P

ITERS = 3
TEACHER_TEMP = 0.07
STUDENT_TEMP = 0.1
LOG2E = 1.4426950408889634

YN = 4
TILE = 512
LANES = 128
MESH = pl.DeviceIdType.MESH
f32 = jnp.float32
bf16 = jnp.bfloat16


def mm(a, b):
    return jnp.dot(a, b, preferred_element_type=f32)


def mm_t(a, b):
    return lax.dot_general(a, b, (((1,), (1,)), ((), ())), preferred_element_type=f32)


def split(v):
    hi = v.astype(bf16)
    return hi, (v - hi.astype(f32)).astype(bf16)


def kernel(
    SN,
    PN,
    t_hbm,
    s_hbm,
    p_hbm,
    gf_out,
    gp_out,
    feats,
    thh,
    tl,
    shh,
    sl,
    st,
    phl,
    e,
    q,
    dh,
    dl,
    cola,
    cola_in,
    col,
    col_in,
    pscale,
    peakf,
    acc,
    mx,
    cb,
    ab,
    rowm,
    row_in,
    stat,
    stat_in,
    gfacc,
    gfs,
    gya,
    gyb,
    gfz,
    gft,
    gfz2,
    gfo,
    cr,
    xa,
    xb,
    load_sem,
    cs_sem,
    cr_sem,
    rs_sem,
    rr_sem,
    st_sem,
    ys_sem,
    yr_sem,
    zs_sem,
    zr_sem,
    ks_sem,
    kr_sem,
    xs_sem,
    xr_sem,
    enter_sem,
    wa,
    wb,
):
    ZN = PN // YN
    XN = SN // 2
    rows, width = t_hbm.shape
    tiles = p_hbm.shape[1] // TILE
    per = TILE // LANES
    blocks = rows // LANES
    s = lax.axis_index("smp")
    p = lax.axis_index("proto")
    x = s // 2
    c = s % 2
    z = p // YN
    y = p % YN
    sibling = (2 * x + 1 - c, p)
    right = (2 * ((x + 1) % XN) + c, p)
    left = (2 * ((x + XN - 1) % XN) + c, p)
    y_right = (s, z * YN + (y + 1) % YN)
    y_left = (s, z * YN + (y + YN - 1) % YN)

    def far(d, n):
        return min(d, n - d)

    offsets = sorted(((dx, dc) for dx in range(XN) for dc in range(2)), key=lambda o: -far(o[0], XN))
    smp_peers = [2 * ((x + dx) % XN) + (c + dc) % 2 for dx, dc in offsets if dx or dc]
    smp_group = (s, SN, [(k, (k, p)) for k in smp_peers])
    offsets = sorted(((dz, dy) for dz in range(ZN) for dy in range(YN)), key=lambda o: -far(o[0], ZN) - far(o[1], YN))
    row_peers = [((z + dz) % ZN) * YN + (y + dy) % YN for dz, dy in offsets if dz or dy]
    row_group = (p, PN, [(k, (s, k)) for k in row_peers])
    z_peers = [(z + dz) % ZN for dz in sorted(range(1, ZN), key=lambda d: -far(d, ZN))]
    z_group = (z, ZN, [(k, (s, k * YN + y)) for k in z_peers])

    def rc(src, dst, ss, rs, dev):
        return pltpu.make_async_remote_copy(
            src_ref=src, dst_ref=dst, send_sem=ss, recv_sem=rs, device_id=dev, device_id_type=MESH
        )

    load_t = pltpu.make_async_copy(t_hbm, feats.at[0], load_sem.at[0])
    load_s = pltpu.make_async_copy(s_hbm, feats.at[1], load_sem.at[1])

    def load_p(j):
        cols = pl.ds(pl.multiple_of(j * TILE, TILE), TILE)
        return pltpu.make_async_copy(
            p_hbm.at[:, cols], q.at[j, pl.ds(0, width)], load_sem.at[2 + j]
        )

    load_t.start()
    for j in range(tiles):
        load_p(j).start()
    load_s.start()

    barrier = pltpu.get_barrier_semaphore()
    y_peers = [(s, z * YN + (y + dy) % YN) for dy in range(1, YN)]
    greet = [dev for _, dev in z_group[2]] + y_peers + [dev for _, dev in smp_group[2]]
    for dev in greet:
        pl.semaphore_signal(barrier, inc=1, device_id=dev, device_id_type=MESH)

    def enter_start():
        pl.semaphore_wait(barrier, len(greet))
        for dev in y_peers:
            pl.semaphore_signal(enter_sem, inc=1, device_id=dev, device_id_type=MESH)

    def enter_wait():
        pl.semaphore_wait(enter_sem, len(y_peers))

    def group_send(src, dst, group, ssem, rsem):
        me, n, peers = group
        for k, dev in peers:
            rc(src(k), dst.at[me], ssem, rsem, dev).start()

    def group_wait(dst, group, ssem, rsem):
        me, n, peers = group
        blocks = dst.at[pl.ds(0, n - 1)]
        copy = rc(blocks, blocks, ssem, rsem, peers[0][1])
        copy.wait_recv()
        copy.wait_send()

    load_t.wait()
    hi, lo = split(feats[0] * (LOG2E / (TEACHER_TEMP / STUDENT_TEMP)))
    thh[:, 0:width] = hi
    thh[:, width : 2 * width] = hi
    tl[...] = lo

    @pl.loop(0, tiles)
    def _(j):
        load_p(j).wait()
        ph, plo = split(q[j, 0:width, :] * (1.0 / STUDENT_TEMP))
        phl[j, 0:width, :] = ph
        phl[j, width : 2 * width, :] = plo
        scores = mm(thh[...], phl[j]) + mm(tl[...], phl[j, 0:width, :])
        top = jnp.max(scores, axis=0, keepdims=True)
        ex = jnp.exp2(scores - top)
        e[j] = ex
        total = jnp.sum(ex, axis=0, keepdims=True)
        for i in range(per):
            cola[pl.ds(per * j + i, 1), :] = top[:, LANES * i : LANES * (i + 1)]
            cola[pl.ds(per * (tiles + j) + i, 1), :] = total[:, LANES * i : LANES * (i + 1)]

    enter_start()

    def student(first, last):
        @pl.loop(first, last)
        def _(j):
            scores = mm(shh[...], phl[j]) + mm(sl[...], phl[j, 0:width, :])
            q[j] = scores
            for r in range(blocks):
                rs = slice(LANES * r, LANES * (r + 1))
                m = mx[rs, :]
                for i in range(per):
                    m = jnp.maximum(m, scores[rs, LANES * i : LANES * (i + 1)])
                mx[rs, :] = m

    def student_start():
        load_s.wait()
        sf = feats[1]
        shi, slo = split(sf * LOG2E)
        shh[:, 0:width] = shi
        shh[:, width : 2 * width] = shi
        sl[...] = slo
        mx[...] = jnp.full(mx.shape, -jnp.inf, f32)

    def student_transpose():
        keep = width // SN
        ht, lt = split((feats[1] * (1.0 / STUDENT_TEMP)).T)
        for core in range(2):
            for chip in range(XN):
                to = (core * XN + chip) * keep
                fr = (2 * chip + core) * keep
                st[0, to : to + keep, :] = ht[fr : fr + keep, :]
                st[1, to : to + keep, :] = lt[fr : fr + keep, :]

    def to_rows(ref, reduce, out, base):
        for r in range(blocks):
            rs = slice(LANES * r, LANES * (r + 1))
            out[base + r : base + r + 1, :] = reduce(ref[rs, :].T, axis=0, keepdims=True)

    def to_columns(v, out):
        for r in range(blocks):
            rs = slice(LANES * r, LANES * (r + 1))
            out[rs, :] = jnp.broadcast_to(v[r : r + 1, :], (LANES, LANES)).T

    def student_totals():
        to_rows(mx, jnp.max, stat, 0)
        to_columns(stat[0:blocks, :], ab)
        mx[...] = jnp.zeros(mx.shape, f32)

        @pl.loop(0, tiles)
        def _(j):
            for r in range(blocks):
                rs = slice(LANES * r, LANES * (r + 1))
                m = ab[rs, :]
                a = mx[rs, :]
                for i in range(per):
                    ls = slice(LANES * i, LANES * (i + 1))
                    v = jnp.exp2(q[j, rs, ls] - m)
                    q[j, rs, ls] = v
                    a = a + v
                mx[rs, :] = a

        to_rows(mx, jnp.sum, stat, blocks)

    def row_pass(it):
        acc[...] = jnp.zeros(acc.shape, f32)

        @pl.loop(0, tiles)
        def _(j):
            ws = [pscale[pl.ds(per * j + i, 1), :] for i in range(per)]
            fs = [peakf[pl.ds(per * j + i, 1), :] for i in range(per)] if it == 0 else None
            for r in range(blocks):
                rs = slice(LANES * r, LANES * (r + 1))
                a = acc[rs, :]
                for i in range(per):
                    ls = slice(LANES * i, LANES * (i + 1))
                    v = e[j, rs, ls]
                    if it == 0:
                        v = v * fs[i]
                        e[j, rs, ls] = v
                    a = a + v * ws[i]
                acc[rs, :] = a

        to_rows(acc, jnp.sum, rowm.at[it], 0)

    def row_start(it):
        row_in[it, pl.ds(p, 1)] = rowm[it : it + 1]
        group_send(lambda k: rowm.at[it], row_in.at[it], row_group, rs_sem.at[it], rr_sem.at[it])

    def row_end(it):
        group_wait(row_in.at[it], row_group, rs_sem.at[it], rr_sem.at[it])
        mass = sum(row_in[it, k] for k in range(PN))
        to_columns(1.0 / mass, cb)

    def col_pass(it):
        @pl.loop(0, tiles)
        def _(j):
            for i in range(per):
                ls = slice(LANES * i, LANES * (i + 1))
                v = jnp.sum(e[j, :, ls] * cb[...], axis=0, keepdims=True)
                col[it, pl.ds(per * j + i, 1), :] = v

    def col_start(it):
        col_in[it, pl.ds(s, 1)] = col[it : it + 1]
        group_send(lambda k: col.at[it], col_in.at[it], smp_group, cs_sem.at[it + 1], cr_sem.at[it + 1])

    def col_end(it):
        group_wait(col_in.at[it], smp_group, cs_sem.at[it + 1], cr_sem.at[it + 1])
        pscale[...] = 1.0 / sum(col_in[it, k] for k in range(SN))

    keep = width // SN
    hk = keep // 2
    mine = pl.multiple_of(c * (width // 2), width // 2)
    other = pl.multiple_of((1 - c) * (width // 2), width // 2)
    across = pl.multiple_of(((x + 2) % XN) * keep, keep)
    ahead = pl.multiple_of(((x + 1) % XN) * keep, keep)
    behind = pl.multiple_of(((x + XN - 1) % XN) * keep, keep)
    here = pl.multiple_of(x * keep, keep)

    def core_copy(t):
        return rc(e.at[t, pl.ds(other, width // 2)], cr.at[t], ks_sem.at[t], kr_sem.at[t], sibling)

    def x_copy(t, k):
        row, dst, dev = [
            (across, xa.at[t, 0], right),
            (across + hk, xa.at[t, 1], left),
            (ahead + hk, xb.at[t, 0, pl.ds(hk, hk)], right),
            (behind, xb.at[t, 1, pl.ds(0, hk)], left),
            (ahead, xb.at[t, 0, pl.ds(0, hk)], right),
            (behind + hk, xb.at[t, 1, pl.ds(hk, hk)], left),
        ][k]
        src = cr.at[t, pl.ds(pl.multiple_of(row, 8), hk)]
        return rc(src, dst, xs_sem.at[t, k], xr_sem.at[t, k], dev)

    def gp_terms(t):
        d = dh[t]
        e[t, 0:width, :] = mm(st[0], d) + mm(st[1], d) + mm(st[0], dl[t])
        core_copy(t).start()

    def gp_core(t):
        core_copy(t).wait_recv()
        cr[t] = cr[t] + e[t, pl.ds(mine, width // 2), :]
        x_copy(t, 0).start()
        x_copy(t, 1).start()

        @pl.when(t < 2)
        def _():
            x_copy(t, 2).start()
            x_copy(t, 3).start()

    def gp_relay(t):
        x_copy(t, 0).wait_recv()
        x_copy(t, 1).wait_recv()
        a = pl.ds(pl.multiple_of(ahead, 8), hk)
        cr[t, a, :] = cr[t, a, :] + xa[t, 0]
        b = pl.ds(pl.multiple_of(behind + hk, 8), hk)
        cr[t, b, :] = cr[t, b, :] + xa[t, 1]

        @pl.when(t >= 2)
        def _():
            x_copy(t, 2).start()
            x_copy(t, 3).start()

        x_copy(t, 4).start()
        x_copy(t, 5).start()

    def gp_end(t):
        for k in range(2, 6):
            x_copy(t, k).wait_recv()
        cols = pl.ds(pl.multiple_of(t * TILE, TILE), TILE)
        gp_out[:, cols] = cr[t, pl.ds(here, keep), :] + xb[t, 0] + xb[t, 1]
        core_copy(t).wait_send()
        for k in range(6):
            x_copy(t, k).wait_send()

    part = rows // 2
    chunk = part // YN
    hc = chunk // 2
    piece = chunk // ZN

    def chunk_at(r, d, low, size):
        return pl.ds(pl.multiple_of((r % 2) * part + ((y + d) % YN) * chunk + low, 8), size)

    def y_copy(r, k):
        d, low, dst, dev = [
            (2, 0, gya.at[r, 0], y_right),
            (2, hc, gya.at[r, 1], y_left),
            (1, hc, gyb.at[r, 0, pl.ds(hc, hc)], y_right),
            (YN - 1, 0, gyb.at[r, 1, pl.ds(0, hc)], y_left),
            (1, 0, gyb.at[r, 0, pl.ds(0, hc)], y_right),
            (YN - 1, hc, gyb.at[r, 1, pl.ds(hc, hc)], y_left),
        ][k]
        return rc(gfs.at[r // 2, chunk_at(r, d, low, hc)], dst, ys_sem.at[r, k], yr_sem.at[r, k], dev)

    def y_gather(r, k):
        d, low, size, dev = [
            (0, 0, chunk, y_right),
            (0, 0, chunk, y_left),
            (YN - 1, 0, hc, y_right),
            (1, hc, hc, y_left),
        ][k]
        src = gfo.at[chunk_at(r, d, low, size)]
        return rc(src, src, ys_sem.at[r, 6 + k], yr_sem.at[r, 6 + k], dev)

    def y_arrive(r, k):
        d, low, size = [(YN - 1, 0, chunk), (1, 0, chunk), (2, 0, hc), (2, hc, hc)][k]
        dst = gfo.at[chunk_at(r, d, low, size)]
        rc(dst, dst, ys_sem.at[r, 6 + k], yr_sem.at[r, 6 + k], y_right).wait_recv()

    def gf_a(r):
        for k in range(4):
            y_copy(r, k).start()

    def gf_b(r):
        for k in range(2):
            y_copy(r, k).wait_recv()
        a = chunk_at(r, 1, 0, hc)
        gfs[r // 2, a, :] = gfs[r // 2, a, :] + gya[r, 0]
        b = chunk_at(r, YN - 1, hc, hc)
        gfs[r // 2, b, :] = gfs[r // 2, b, :] + gya[r, 1]
        y_copy(r, 4).start()
        y_copy(r, 5).start()

    def gf_c(r):
        for k in range(2, 6):
            y_copy(r, k).wait_recv()
        for k in range(ZN):
            rs = slice(k * piece, (k + 1) * piece)
            own = gfs[r // 2, chunk_at(r, 0, k * piece, piece), :]
            gft[r, k] = own + gyb[r, 0, rs, :] + gyb[r, 1, rs, :]
        group_send(lambda k: gft.at[r, k], gfz.at[r], z_group, zs_sem.at[r], zr_sem.at[r])

    def gf_d(r):
        group_wait(gfz.at[r], z_group, zs_sem.at[r], zr_sem.at[r])
        gfz[r, pl.ds(z, 1)] = gft[r, pl.ds(z, 1)]
        if r < 2:
            targets = sum(gfz[r, k] for k in range(ZN))
            probs = sum(gfz[r + 2, k] for k in range(ZN))
            scale = cb[chunk_at(r, 0, z * piece, piece), :]
            scale = jnp.concatenate([scale] * (width // LANES), axis=1)
            gfz2[r, pl.ds(z, 1)] = (probs - scale * targets)[None]
            group_send(lambda k: gfz2.at[r, z], gfz2.at[r], z_group, zs_sem.at[4 + r], zr_sem.at[4 + r])

    def gf_e(r):
        group_wait(gfz2.at[r], z_group, zs_sem.at[4 + r], zr_sem.at[4 + r])
        for k in range(ZN):
            gfo[chunk_at(r, 0, k * piece, piece), :] = gfz2[r, k]
        y_gather(r, 0).start()
        y_gather(r, 1).start()

    def gf_f(r):
        y_arrive(r, 0)
        y_arrive(r, 1)
        y_gather(r, 2).start()
        y_gather(r, 3).start()

    def gf_g(r):
        y_arrive(r, 2)
        y_arrive(r, 3)
        rs = pl.ds(r * part, part)
        gf_out[rs, :] = gfo[rs, :]
        for k in range(6):
            y_copy(r, k).wait_send()
            y_copy(r + 2, k).wait_send()
        for k in range(4):
            y_gather(r, k).wait_send()

    def feat_terms(j, which, rs):
        gfacc[which, rs, :] += mm_t(dh[j, rs, :], phl[j])
        gfacc[which, rs, 0:width] += mm_t(dl[j, rs, :], phl[j, 0:width, :])

    everything = slice(0, rows)
    halves = [slice(0, part), slice(part, rows)]

    def probs_terms(first, last):
        @pl.loop(first, last)
        def _(j):
            hi, lo = split(q[j])
            dh[j] = hi
            dl[j] = lo
            feat_terms(j, 1, everything)

    def probs_sum():
        for k in range(width // LANES):
            ls = slice(LANES * k, LANES * (k + 1))
            us = slice(width + LANES * k, width + LANES * (k + 1))
            gfs[1, :, ls] = (gfacc[1, :, ls] + gfacc[1, :, us]) * ab[...]
        gf_a(2)
        gf_a(3)

    def mass_tile(j, out):
        for k in range(per):
            ls = slice(LANES * k, LANES * (k + 1))
            hi, lo = split(e[j, :, ls] * pscale[pl.ds(per * j + k, 1), :])
            out[0, :, ls] = hi
            out[1, :, ls] = lo

    def mass_add(j, tile):
        gfacc[0] += mm_t(tile[0], phl[j])
        gfacc[0, :, 0:width] += mm_t(tile[1], phl[j, 0:width, :])

    def mass_terms():
        mass_tile(0, wa)

        @pl.loop(0, tiles // 2)
        def _(i):
            mass_tile(2 * i + 1, wb)
            mass_add(2 * i, wa)
            mass_tile((2 * i + 2) % tiles, wa)
            mass_add(2 * i + 1, wb)

    def mass_sum(h):
        rs = halves[h]
        gfs[0, rs, :] = gfacc[0, rs, 0:width] + gfacc[0, rs, width : 2 * width]
        gf_a(h)

    half = per * tiles
    cola_in[pl.ds(s, 1)] = cola[...][None]
    group_send(lambda k: cola, cola_in, smp_group, cs_sem.at[0], cr_sem.at[0])
    student_start()
    student(0, 5)
    gfacc[...] = jnp.zeros(gfacc.shape, f32)
    group_wait(cola_in, smp_group, cs_sem.at[0], cr_sem.at[0])
    tops = [cola_in[k, 0:half, :] for k in range(SN)]
    top = functools.reduce(jnp.maximum, tops)
    pscale[...] = 1.0 / sum(cola_in[k, half : 2 * half, :] * jnp.exp2(tops[k] - top) for k in range(SN))
    peakf[...] = jnp.exp2(cola[0:half, :] - top)

    row_pass(0)
    enter_wait()
    row_start(0)
    student(5, tiles)
    student_totals()
    row_end(0)
    col_pass(0)
    col_start(0)
    stat_in[pl.ds(p, 1)] = stat[...][None]
    group_send(lambda k: stat, stat_in, row_group, st_sem.at[0], st_sem.at[1])
    probs_terms(0, 4)
    col_end(0)

    row_pass(1)
    row_start(1)
    probs_terms(4, tiles)
    group_wait(stat_in, row_group, st_sem.at[0], st_sem.at[1])
    tops = [stat_in[k, 0:blocks, :] for k in range(PN)]
    top = functools.reduce(jnp.maximum, tops)
    total = sum(stat_in[k, blocks : 2 * blocks, :] * jnp.exp2(tops[k] - top) for k in range(PN))
    to_columns(jnp.exp2(stat[0:blocks, :] - top) / total, ab)
    row_end(1)
    col_pass(1)
    col_start(1)
    probs_sum()
    student_transpose()
    col_end(1)

    row_pass(2)
    row_start(2)
    gf_b(2)
    gf_b(3)
    mass_terms()
    mass_sum(0)
    mass_sum(1)
    row_end(2)

    lag_core, lag_relay, lag_end = 2, 6, 10
    at = {
        2: [(gf_c, 2), (gf_c, 3)],
        3: [(gf_b, 0)],
        4: [(gf_b, 1)],
        5: [(gf_c, 0)],
        6: [(gf_c, 1)],
        7: [(gf_d, 2), (gf_d, 3)],
        9: [(gf_d, 0)],
        11: [(gf_d, 1)],
        12: [(gf_e, 0)],
        13: [(gf_e, 1)],
        14: [(gf_f, 0)],
        15: [(gf_f, 1)],
        16: [(gf_g, 0)],
        17: [(gf_g, 1)],
    }

    def dlogits(i):
        for k in range(per):
            ls = slice(LANES * k, LANES * (k + 1))
            w = pscale[pl.ds(per * i + k, 1), :]
            d = q[i, :, ls] * ab[...] - (cb[...] * e[i, :, ls]) * w
            dhi, dlo = split(d)
            dh[i, :, ls] = dhi
            dl[i, :, ls] = dlo

    @pl.loop(0, 2)
    def _(i):
        dlogits(i)
        gp_terms(i)


    @pl.loop(2, tiles + lag_end)
    def _(i):
        @pl.when(i < tiles)
        def _():
            dlogits(i)
            gp_terms(i)

        @pl.when((i >= lag_core) & (i < tiles + lag_core))
        def _():
            gp_core(i - lag_core)

        @pl.when((i >= lag_relay) & (i < tiles + lag_relay))
        def _():
            gp_relay(i - lag_relay)

        for when, todo in at.items():

            @pl.when(i == when)
            def _(todo=todo):
                for f, h in todo:
                    f(h)

        @pl.when(i >= lag_end)
        def _():
            gp_end(i - lag_end)


def finish(gf_in, gp_in, gf_out, gp_out, sem):
    copies = []
    for k, (src, dst) in enumerate(((gf_in, gf_out), (gp_in, gp_out))):
        n = src.shape[0] // 2
        for h in range(2):
            rs = pl.ds(h * n, n)
            copies.append(pltpu.make_async_copy(src.at[rs], dst.at[rs], sem.at[2 * k + h]))
    for copy in copies:
        copy.start()
    for copy in copies:
        copy.wait()


def local(SN, PN, teacher_feats, student_feats, prototypes):
    rows, width = teacher_feats.shape
    protos = prototypes.shape[1]
    tiles = protos // TILE
    half = protos // LANES
    blocks = rows // LANES
    ZN = PN // YN
    chunk = rows // 2 // YN
    piece = chunk // ZN
    V = pltpu.VMEM
    DMA = pltpu.SemaphoreType.DMA
    scratch = [
        V((2, rows, width), f32),
        V((rows, 2 * width), bf16),
        V((rows, width), bf16),
        V((rows, 2 * width), bf16),
        V((rows, width), bf16),
        V((2, width, rows), bf16),
        V((tiles, 2 * width, TILE), bf16),
        V((tiles, rows, TILE), f32),
        V((tiles, rows, TILE), f32),
        V((tiles, rows, TILE), bf16),
        V((tiles, rows, TILE), bf16),
        V((2 * half, LANES), f32),
        V((SN, 2 * half, LANES), f32),
        V((ITERS - 1, half, LANES), f32),
        V((ITERS - 1, SN, half, LANES), f32),
        V((half, LANES), f32),
        V((half, LANES), f32),
        V((rows, LANES), f32),
        V((rows, LANES), f32),
        V((rows, LANES), f32),
        V((rows, LANES), f32),
        V((ITERS, blocks, LANES), f32),
        V((ITERS, PN, blocks, LANES), f32),
        V((2 * blocks, LANES), f32),
        V((PN, 2 * blocks, LANES), f32),
        V((2, rows, 2 * width), f32),
        V((2, rows, width), f32),
        V((4, 2, chunk // 2, width), f32),
        V((4, 2, chunk, width), f32),
        V((4, ZN, piece, width), f32),
        V((4, ZN, piece, width), f32),
        V((2, ZN, piece, width), f32),
        V((rows, width), f32),
        V((tiles, width // 2, TILE), f32),
        V((tiles, 2, width // SN // 2, TILE), f32),
        V((tiles, 2, width // SN, TILE), f32),
        DMA((2 + tiles,)),
        DMA((ITERS,)),
        DMA((ITERS,)),
        DMA((ITERS,)),
        DMA((ITERS,)),
        DMA((2,)),
        DMA((4, 10)),
        DMA((4, 10)),
        DMA((6,)),
        DMA((6,)),
        DMA((tiles,)),
        DMA((tiles,)),
        DMA((tiles, 6)),
        DMA((tiles, 6)),
        pltpu.SemaphoreType.REGULAR,
        V((2, rows, TILE), bf16),
        V((2, rows, TILE), bf16),
    ]
    flops = 2 * rows * width * protos
    shapes = (
        jax.ShapeDtypeStruct((rows, width), f32),
        jax.ShapeDtypeStruct((width // SN, protos), f32),
    )
    outs = pl.pallas_call(
        functools.partial(kernel, SN, PN),
        out_shape=tuple(V(o.shape, o.dtype) for o in shapes),
        in_specs=[pl.BlockSpec(memory_space=pl.ANY)] * 3,
        out_specs=(pl.BlockSpec(memory_space=pltpu.VMEM),) * 2,
        scratch_shapes=scratch,
        compiler_params=pltpu.CompilerParams(
            collective_id=0, has_side_effects=True, vmem_limit_bytes=60 * 1024 * 1024
        ),
        cost_estimate=pl.CostEstimate(
            flops=12 * flops, bytes_accessed=4 * width * (protos + 4 * rows), transcendentals=2 * rows * protos
        ),
    )(teacher_feats, student_feats, prototypes)
    return pl.pallas_call(
        finish,
        out_shape=shapes,
        in_specs=[pl.BlockSpec(memory_space=pltpu.VMEM)] * 2,
        out_specs=(pl.BlockSpec(memory_space=pl.ANY),) * 2,
        scratch_shapes=[DMA((4,))],
        compiler_params=pltpu.CompilerParams(vmem_limit_bytes=4 * 1024 * 1024),
        cost_estimate=pl.CostEstimate(
            flops=0, bytes_accessed=8 * (rows * width + width // SN * protos), transcendentals=0
        ),
    )(*outs)


def solution(mesh):
    SN, PN = mesh.shape["smp"], mesh.shape["proto"]
    in_specs = (P("smp", None), P("smp", None), P(None, "proto"))
    out_specs = (P("smp", None), P("smp", "proto"))
    return jax.shard_map(
        functools.partial(local, SN, PN), mesh=mesh, in_specs=in_specs, out_specs=out_specs, check_vma=False
    )
```

```python
import functools

import jax
import jax.numpy as jnp
from jax import lax
from jax.experimental import pallas as pl
from jax.experimental.pallas import tpu as pltpu
from jax.sharding import PartitionSpec as P

ITERS = 3
TEACHER_TEMP = 0.07
STUDENT_TEMP = 0.1
LOG2E = 1.4426950408889634

YN = 4
TILE = 512
LANES = 128
MESH = pl.DeviceIdType.MESH
f32 = jnp.float32
bf16 = jnp.bfloat16


def mm(a, b):
    return jnp.dot(a, b, preferred_element_type=f32)


def mm_t(a, b):
    return lax.dot_general(a, b, (((1,), (1,)), ((), ())), preferred_element_type=f32)


def split(v):
    hi = v.astype(bf16)
    return hi, (v - hi.astype(f32)).astype(bf16)


def kernel(
    SN,
    PN,
    t_hbm,
    s_hbm,
    p_hbm,
    gf_out,
    gp_out,
    feats,
    thh,
    tl,
    shh,
    sl,
    st,
    phl,
    e,
    q,
    dh,
    dl,
    cola,
    cola_in,
    col,
    col_in,
    pscale,
    peakf,
    acc,
    mx,
    cb,
    ab,
    rowm,
    row_in,
    stat,
    stat_in,
    gfacc,
    gfs,
    gya,
    gyb,
    gfz,
    gft,
    gfz2,
    gfo,
    cr,
    xa,
    xb,
    load_sem,
    cs_sem,
    cr_sem,
    rs_sem,
    rr_sem,
    st_sem,
    ys_sem,
    yr_sem,
    zs_sem,
    zr_sem,
    ks_sem,
    kr_sem,
    xs_sem,
    xr_sem,
    enter_sem,
    wa,
    wb,
    sa,
    sb,
):
    ZN = PN // YN
    XN = SN // 2
    rows, width = t_hbm.shape
    tiles = p_hbm.shape[1] // TILE
    per = TILE // LANES
    blocks = rows // LANES
    s = lax.axis_index("smp")
    p = lax.axis_index("proto")
    x = s // 2
    c = s % 2
    z = p // YN
    y = p % YN
    sibling = (2 * x + 1 - c, p)
    right = (2 * ((x + 1) % XN) + c, p)
    left = (2 * ((x + XN - 1) % XN) + c, p)
    y_right = (s, z * YN + (y + 1) % YN)
    y_left = (s, z * YN + (y + YN - 1) % YN)

    def far(d, n):
        return min(d, n - d)

    offsets = sorted(((dx, dc) for dx in range(XN) for dc in range(2)), key=lambda o: -far(o[0], XN))
    smp_peers = [2 * ((x + dx) % XN) + (c + dc) % 2 for dx, dc in offsets if dx or dc]
    smp_group = (s, SN, [(k, (k, p)) for k in smp_peers])
    offsets = sorted(((dz, dy) for dz in range(ZN) for dy in range(YN)), key=lambda o: -far(o[0], ZN) - far(o[1], YN))
    row_peers = [((z + dz) % ZN) * YN + (y + dy) % YN for dz, dy in offsets if dz or dy]
    row_group = (p, PN, [(k, (s, k)) for k in row_peers])
    z_peers = [(z + dz) % ZN for dz in sorted(range(1, ZN), key=lambda d: -far(d, ZN))]
    z_group = (z, ZN, [(k, (s, k * YN + y)) for k in z_peers])

    def rc(src, dst, ss, rs, dev):
        return pltpu.make_async_remote_copy(
            src_ref=src, dst_ref=dst, send_sem=ss, recv_sem=rs, device_id=dev, device_id_type=MESH
        )

    load_t = pltpu.make_async_copy(t_hbm, feats.at[0], load_sem.at[0])
    load_s = pltpu.make_async_copy(s_hbm, feats.at[1], load_sem.at[1])

    def load_p(j):
        cols = pl.ds(pl.multiple_of(j * TILE, TILE), TILE)
        return pltpu.make_async_copy(
            p_hbm.at[:, cols], q.at[j, pl.ds(0, width)], load_sem.at[2 + j]
        )

    load_t.start()
    for j in range(tiles):
        load_p(j).start()
    load_s.start()

    barrier = pltpu.get_barrier_semaphore()
    y_peers = [(s, z * YN + (y + dy) % YN) for dy in range(1, YN)]
    greet = [dev for _, dev in z_group[2]] + y_peers + [dev for _, dev in smp_group[2]]
    for dev in greet:
        pl.semaphore_signal(barrier, inc=1, device_id=dev, device_id_type=MESH)

    def enter_start():
        pl.semaphore_wait(barrier, len(greet))
        for dev in y_peers:
            pl.semaphore_signal(enter_sem, inc=1, device_id=dev, device_id_type=MESH)

    def enter_wait():
        pl.semaphore_wait(enter_sem, len(y_peers))

    def group_send(src, dst, group, ssem, rsem):
        me, n, peers = group
        for k, dev in peers:
            rc(src(k), dst.at[me], ssem, rsem, dev).start()

    def group_wait(dst, group, ssem, rsem):
        me, n, peers = group
        blocks = dst.at[pl.ds(0, n - 1)]
        copy = rc(blocks, blocks, ssem, rsem, peers[0][1])
        copy.wait_recv()
        copy.wait_send()

    load_t.wait()
    hi, lo = split(feats[0] * (LOG2E / (TEACHER_TEMP / STUDENT_TEMP)))
    thh[:, 0:width] = hi
    thh[:, width : 2 * width] = hi
    tl[...] = lo

    def teacher_split(j):
        ph, plo = split(q[j, 0:width, :] * (1.0 / STUDENT_TEMP))
        phl[j, 0:width, :] = ph
        phl[j, width : 2 * width, :] = plo

    def teacher_scores(j, out):
        out[...] = mm(thh[...], phl[j]) + mm(tl[...], phl[j, 0:width, :])

    def teacher_expo(j, scores):
        top = jnp.max(scores[...], axis=0, keepdims=True)
        ex = jnp.exp2(scores[...] - top)
        e[j] = ex
        total = jnp.sum(ex, axis=0, keepdims=True)
        for i in range(per):
            cola[pl.ds(per * j + i, 1), :] = top[:, LANES * i : LANES * (i + 1)]
            cola[pl.ds(per * (tiles + j) + i, 1), :] = total[:, LANES * i : LANES * (i + 1)]

    load_p(0).wait()
    load_p(1).wait()
    teacher_split(0)
    teacher_split(1)
    teacher_scores(0, sa)

    @pl.loop(0, tiles // 2 - 1)
    def _(i):
        j = 2 * i + 1
        load_p(j + 1).wait()
        load_p(j + 2).wait()
        teacher_scores(j, sb)
        teacher_expo(j - 1, sa)
        teacher_split(j + 1)
        teacher_scores(j + 1, sa)
        teacher_expo(j, sb)
        teacher_split(j + 2)

    teacher_scores(tiles - 1, sb)
    teacher_expo(tiles - 2, sa)
    teacher_expo(tiles - 1, sb)

    enter_start()

    def student(first, last):
        @pl.loop(first, last)
        def _(j):
            scores = mm(shh[...], phl[j]) + mm(sl[...], phl[j, 0:width, :])
            q[j] = scores
            for r in range(blocks):
                rs = slice(LANES * r, LANES * (r + 1))
                m = mx[rs, :]
                for i in range(per):
                    m = jnp.maximum(m, scores[rs, LANES * i : LANES * (i + 1)])
                mx[rs, :] = m

    def student_start():
        load_s.wait()
        sf = feats[1]
        shi, slo = split(sf * LOG2E)
        shh[:, 0:width] = shi
        shh[:, width : 2 * width] = shi
        sl[...] = slo
        mx[...] = jnp.full(mx.shape, -jnp.inf, f32)

    def student_transpose():
        keep = width // SN
        ht, lt = split((feats[1] * (1.0 / STUDENT_TEMP)).T)
        for core in range(2):
            for chip in range(XN):
                to = (core * XN + chip) * keep
                fr = (2 * chip + core) * keep
                st[0, to : to + keep, :] = ht[fr : fr + keep, :]
                st[1, to : to + keep, :] = lt[fr : fr + keep, :]

    def to_rows(ref, reduce, out, base):
        for r in range(blocks):
            rs = slice(LANES * r, LANES * (r + 1))
            out[base + r : base + r + 1, :] = reduce(ref[rs, :].T, axis=0, keepdims=True)

    def to_columns(v, out):
        for r in range(blocks):
            rs = slice(LANES * r, LANES * (r + 1))
            out[rs, :] = jnp.broadcast_to(v[r : r + 1, :], (LANES, LANES)).T

    def student_totals():
        to_rows(mx, jnp.max, stat, 0)
        to_columns(stat[0:blocks, :], ab)
        mx[...] = jnp.zeros(mx.shape, f32)

        @pl.loop(0, tiles)
        def _(j):
            for r in range(blocks):
                rs = slice(LANES * r, LANES * (r + 1))
                m = ab[rs, :]
                a = mx[rs, :]
                for i in range(per):
                    ls = slice(LANES * i, LANES * (i + 1))
                    v = jnp.exp2(q[j, rs, ls] - m)
                    q[j, rs, ls] = v
                    a = a + v
                mx[rs, :] = a

        to_rows(mx, jnp.sum, stat, blocks)

    def row_pass(it):
        acc[...] = jnp.zeros(acc.shape, f32)

        @pl.loop(0, tiles)
        def _(j):
            ws = [pscale[pl.ds(per * j + i, 1), :] for i in range(per)]
            fs = [peakf[pl.ds(per * j + i, 1), :] for i in range(per)] if it == 0 else None
            for r in range(blocks):
                rs = slice(LANES * r, LANES * (r + 1))
                a = acc[rs, :]
                for i in range(per):
                    ls = slice(LANES * i, LANES * (i + 1))
                    v = e[j, rs, ls]
                    if it == 0:
                        v = v * fs[i]
                        e[j, rs, ls] = v
                    a = a + v * ws[i]
                acc[rs, :] = a

        to_rows(acc, jnp.sum, rowm.at[it], 0)

    def row_start(it):
        row_in[it, pl.ds(p, 1)] = rowm[it : it + 1]
        group_send(lambda k: rowm.at[it], row_in.at[it], row_group, rs_sem.at[it], rr_sem.at[it])

    def row_end(it):
        group_wait(row_in.at[it], row_group, rs_sem.at[it], rr_sem.at[it])
        mass = sum(row_in[it, k] for k in range(PN))
        to_columns(1.0 / mass, cb)

    def col_pass(it):
        @pl.loop(0, tiles)
        def _(j):
            for i in range(per):
                ls = slice(LANES * i, LANES * (i + 1))
                v = jnp.sum(e[j, :, ls] * cb[...], axis=0, keepdims=True)
                col[it, pl.ds(per * j + i, 1), :] = v

    def col_start(it):
        col_in[it, pl.ds(s, 1)] = col[it : it + 1]
        group_send(lambda k: col.at[it], col_in.at[it], smp_group, cs_sem.at[it + 1], cr_sem.at[it + 1])

    def col_end(it):
        group_wait(col_in.at[it], smp_group, cs_sem.at[it + 1], cr_sem.at[it + 1])
        pscale[...] = 1.0 / sum(col_in[it, k] for k in range(SN))

    keep = width // SN
    hk = keep // 2
    mine = pl.multiple_of(c * (width // 2), width // 2)
    other = pl.multiple_of((1 - c) * (width // 2), width // 2)
    across = pl.multiple_of(((x + 2) % XN) * keep, keep)
    ahead = pl.multiple_of(((x + 1) % XN) * keep, keep)
    behind = pl.multiple_of(((x + XN - 1) % XN) * keep, keep)
    here = pl.multiple_of(x * keep, keep)

    def core_copy(t):
        return rc(e.at[t, pl.ds(other, width // 2)], cr.at[t], ks_sem.at[t], kr_sem.at[t], sibling)

    def x_copy(t, k):
        row, dst, dev = [
            (across, xa.at[t, 0], right),
            (across + hk, xa.at[t, 1], left),
            (ahead + hk, xb.at[t, 0, pl.ds(hk, hk)], right),
            (behind, xb.at[t, 1, pl.ds(0, hk)], left),
            (ahead, xb.at[t, 0, pl.ds(0, hk)], right),
            (behind + hk, xb.at[t, 1, pl.ds(hk, hk)], left),
        ][k]
        src = cr.at[t, pl.ds(pl.multiple_of(row, 8), hk)]
        return rc(src, dst, xs_sem.at[t, k], xr_sem.at[t, k], dev)

    def gp_terms(t):
        d = dh[t]
        e[t, 0:width, :] = mm(st[0], d) + mm(st[1], d) + mm(st[0], dl[t])
        core_copy(t).start()

    def gp_core(t):
        core_copy(t).wait_recv()
        cr[t] = cr[t] + e[t, pl.ds(mine, width // 2), :]
        x_copy(t, 0).start()
        x_copy(t, 1).start()

        @pl.when(t < 2)
        def _():
            x_copy(t, 2).start()
            x_copy(t, 3).start()

    def gp_relay(t):
        x_copy(t, 0).wait_recv()
        x_copy(t, 1).wait_recv()
        a = pl.ds(pl.multiple_of(ahead, 8), hk)
        cr[t, a, :] = cr[t, a, :] + xa[t, 0]
        b = pl.ds(pl.multiple_of(behind + hk, 8), hk)
        cr[t, b, :] = cr[t, b, :] + xa[t, 1]

        @pl.when(t >= 2)
        def _():
            x_copy(t, 2).start()
            x_copy(t, 3).start()

        x_copy(t, 4).start()
        x_copy(t, 5).start()

    def gp_end(t):
        for k in range(2, 6):
            x_copy(t, k).wait_recv()
        cols = pl.ds(pl.multiple_of(t * TILE, TILE), TILE)
        gp_out[:, cols] = cr[t, pl.ds(here, keep), :] + xb[t, 0] + xb[t, 1]
        core_copy(t).wait_send()
        for k in range(6):
            x_copy(t, k).wait_send()

    part = rows // 2
    chunk = part // YN
    hc = chunk // 2
    piece = chunk // ZN

    def chunk_at(r, d, low, size):
        return pl.ds(pl.multiple_of((r % 2) * part + ((y + d) % YN) * chunk + low, 8), size)

    def y_copy(r, k):
        d, low, dst, dev = [
            (2, 0, gya.at[r, 0], y_right),
            (2, hc, gya.at[r, 1], y_left),
            (1, hc, gyb.at[r, 0, pl.ds(hc, hc)], y_right),
            (YN - 1, 0, gyb.at[r, 1, pl.ds(0, hc)], y_left),
            (1, 0, gyb.at[r, 0, pl.ds(0, hc)], y_right),
            (YN - 1, hc, gyb.at[r, 1, pl.ds(hc, hc)], y_left),
        ][k]
        return rc(gfs.at[r // 2, chunk_at(r, d, low, hc)], dst, ys_sem.at[r, k], yr_sem.at[r, k], dev)

    def y_gather(r, k):
        d, low, size, dev = [
            (0, 0, chunk, y_right),
            (0, 0, chunk, y_left),
            (YN - 1, 0, hc, y_right),
            (1, hc, hc, y_left),
        ][k]
        src = gfo.at[chunk_at(r, d, low, size)]
        return rc(src, src, ys_sem.at[r, 6 + k], yr_sem.at[r, 6 + k], dev)

    def y_arrive(r, k):
        d, low, size = [(YN - 1, 0, chunk), (1, 0, chunk), (2, 0, hc), (2, hc, hc)][k]
        dst = gfo.at[chunk_at(r, d, low, size)]
        rc(dst, dst, ys_sem.at[r, 6 + k], yr_sem.at[r, 6 + k], y_right).wait_recv()

    def gf_a(r):
        for k in range(4):
            y_copy(r, k).start()

    def gf_b(r):
        for k in range(2):
            y_copy(r, k).wait_recv()
        a = chunk_at(r, 1, 0, hc)
        gfs[r // 2, a, :] = gfs[r // 2, a, :] + gya[r, 0]
        b = chunk_at(r, YN - 1, hc, hc)
        gfs[r // 2, b, :] = gfs[r // 2, b, :] + gya[r, 1]
        y_copy(r, 4).start()
        y_copy(r, 5).start()

    def gf_c(r):
        for k in range(2, 6):
            y_copy(r, k).wait_recv()
        for k in range(ZN):
            rs = slice(k * piece, (k + 1) * piece)
            own = gfs[r // 2, chunk_at(r, 0, k * piece, piece), :]
            gft[r, k] = own + gyb[r, 0, rs, :] + gyb[r, 1, rs, :]
        group_send(lambda k: gft.at[r, k], gfz.at[r], z_group, zs_sem.at[r], zr_sem.at[r])

    def gf_d(r):
        group_wait(gfz.at[r], z_group, zs_sem.at[r], zr_sem.at[r])
        gfz[r, pl.ds(z, 1)] = gft[r, pl.ds(z, 1)]
        if r < 2:
            targets = sum(gfz[r, k] for k in range(ZN))
            probs = sum(gfz[r + 2, k] for k in range(ZN))
            scale = cb[chunk_at(r, 0, z * piece, piece), :]
            scale = jnp.concatenate([scale] * (width // LANES), axis=1)
            gfz2[r, pl.ds(z, 1)] = (probs - scale * targets)[None]
            group_send(lambda k: gfz2.at[r, z], gfz2.at[r], z_group, zs_sem.at[4 + r], zr_sem.at[4 + r])

    def gf_e(r):
        group_wait(gfz2.at[r], z_group, zs_sem.at[4 + r], zr_sem.at[4 + r])
        for k in range(ZN):
            gfo[chunk_at(r, 0, k * piece, piece), :] = gfz2[r, k]
        y_gather(r, 0).start()
        y_gather(r, 1).start()

    def gf_f(r):
        y_arrive(r, 0)
        y_arrive(r, 1)
        y_gather(r, 2).start()
        y_gather(r, 3).start()

    def gf_g(r):
        y_arrive(r, 2)
        y_arrive(r, 3)
        rs = pl.ds(r * part, part)
        gf_out[rs, :] = gfo[rs, :]
        for k in range(6):
            y_copy(r, k).wait_send()
            y_copy(r + 2, k).wait_send()
        for k in range(4):
            y_gather(r, k).wait_send()

    def feat_terms(j, which, rs):
        gfacc[which, rs, :] += mm_t(dh[j, rs, :], phl[j])
        gfacc[which, rs, 0:width] += mm_t(dl[j, rs, :], phl[j, 0:width, :])

    everything = slice(0, rows)
    halves = [slice(0, part), slice(part, rows)]

    def probs_terms(first, last):
        @pl.loop(first, last)
        def _(j):
            hi, lo = split(q[j])
            dh[j] = hi
            dl[j] = lo
            feat_terms(j, 1, everything)

    def probs_sum():
        for k in range(width // LANES):
            ls = slice(LANES * k, LANES * (k + 1))
            us = slice(width + LANES * k, width + LANES * (k + 1))
            gfs[1, :, ls] = (gfacc[1, :, ls] + gfacc[1, :, us]) * ab[...]
        gf_a(2)
        gf_a(3)

    def mass_tile(j, out):
        for k in range(per):
            ls = slice(LANES * k, LANES * (k + 1))
            hi, lo = split(e[j, :, ls] * pscale[pl.ds(per * j + k, 1), :])
            out[0, :, ls] = hi
            out[1, :, ls] = lo

    def mass_add(j, tile):
        gfacc[0] += mm_t(tile[0], phl[j])
        gfacc[0, :, 0:width] += mm_t(tile[1], phl[j, 0:width, :])

    def mass_terms():
        mass_tile(0, wa)

        @pl.loop(0, tiles // 2)
        def _(i):
            mass_tile(2 * i + 1, wb)
            mass_add(2 * i, wa)
            mass_tile((2 * i + 2) % tiles, wa)
            mass_add(2 * i + 1, wb)

    def mass_sum(h):
        rs = halves[h]
        gfs[0, rs, :] = gfacc[0, rs, 0:width] + gfacc[0, rs, width : 2 * width]
        gf_a(h)

    half = per * tiles
    cola_in[pl.ds(s, 1)] = cola[...][None]
    group_send(lambda k: cola, cola_in, smp_group, cs_sem.at[0], cr_sem.at[0])
    student_start()
    student(0, 5)
    gfacc[...] = jnp.zeros(gfacc.shape, f32)
    group_wait(cola_in, smp_group, cs_sem.at[0], cr_sem.at[0])
    tops = [cola_in[k, 0:half, :] for k in range(SN)]
    top = functools.reduce(jnp.maximum, tops)
    pscale[...] = 1.0 / sum(cola_in[k, half : 2 * half, :] * jnp.exp2(tops[k] - top) for k in range(SN))
    peakf[...] = jnp.exp2(cola[0:half, :] - top)

    row_pass(0)
    enter_wait()
    row_start(0)
    student(5, tiles)
    student_totals()
    row_end(0)
    col_pass(0)
    col_start(0)
    stat_in[pl.ds(p, 1)] = stat[...][None]
    group_send(lambda k: stat, stat_in, row_group, st_sem.at[0], st_sem.at[1])
    probs_terms(0, 4)
    col_end(0)

    row_pass(1)
    row_start(1)
    probs_terms(4, tiles)
    group_wait(stat_in, row_group, st_sem.at[0], st_sem.at[1])
    tops = [stat_in[k, 0:blocks, :] for k in range(PN)]
    top = functools.reduce(jnp.maximum, tops)
    total = sum(stat_in[k, blocks : 2 * blocks, :] * jnp.exp2(tops[k] - top) for k in range(PN))
    to_columns(jnp.exp2(stat[0:blocks, :] - top) / total, ab)
    row_end(1)
    col_pass(1)
    col_start(1)
    probs_sum()
    student_transpose()
    col_end(1)

    row_pass(2)
    row_start(2)
    gf_b(2)
    gf_b(3)
    mass_terms()
    mass_sum(0)
    mass_sum(1)
    row_end(2)

    lag_core, lag_relay, lag_end = 2, 6, 10
    at = {
        2: [(gf_c, 2), (gf_c, 3)],
        3: [(gf_b, 0)],
        4: [(gf_b, 1)],
        5: [(gf_c, 0)],
        6: [(gf_c, 1)],
        7: [(gf_d, 2), (gf_d, 3)],
        9: [(gf_d, 0)],
        11: [(gf_d, 1)],
        12: [(gf_e, 0)],
        13: [(gf_e, 1)],
        14: [(gf_f, 0)],
        15: [(gf_f, 1)],
        16: [(gf_g, 0)],
        17: [(gf_g, 1)],
    }

    def dlogits(i):
        for k in range(per):
            ls = slice(LANES * k, LANES * (k + 1))
            w = pscale[pl.ds(per * i + k, 1), :]
            d = q[i, :, ls] * ab[...] - (cb[...] * e[i, :, ls]) * w
            dhi, dlo = split(d)
            dh[i, :, ls] = dhi
            dl[i, :, ls] = dlo

    @pl.loop(0, 2)
    def _(i):
        dlogits(i)
        gp_terms(i)


    @pl.loop(2, tiles + lag_end)
    def _(i):
        @pl.when(i < tiles)
        def _():
            dlogits(i)
            gp_terms(i)

        @pl.when((i >= lag_core) & (i < tiles + lag_core))
        def _():
            gp_core(i - lag_core)

        @pl.when((i >= lag_relay) & (i < tiles + lag_relay))
        def _():
            gp_relay(i - lag_relay)

        for when, todo in at.items():

            @pl.when(i == when)
            def _(todo=todo):
                for f, h in todo:
                    f(h)

        @pl.when(i >= lag_end)
        def _():
            gp_end(i - lag_end)


def finish(gf_in, gp_in, gf_out, gp_out, sem):
    copies = []
    for k, (src, dst) in enumerate(((gf_in, gf_out), (gp_in, gp_out))):
        n = src.shape[0] // 2
        for h in range(2):
            rs = pl.ds(h * n, n)
            copies.append(pltpu.make_async_copy(src.at[rs], dst.at[rs], sem.at[2 * k + h]))
    for copy in copies:
        copy.start()
    for copy in copies:
        copy.wait()


def local(SN, PN, teacher_feats, student_feats, prototypes):
    rows, width = teacher_feats.shape
    protos = prototypes.shape[1]
    tiles = protos // TILE
    half = protos // LANES
    blocks = rows // LANES
    ZN = PN // YN
    chunk = rows // 2 // YN
    piece = chunk // ZN
    V = pltpu.VMEM
    DMA = pltpu.SemaphoreType.DMA
    scratch = [
        V((2, rows, width), f32),
        V((rows, 2 * width), bf16),
        V((rows, width), bf16),
        V((rows, 2 * width), bf16),
        V((rows, width), bf16),
        V((2, width, rows), bf16),
        V((tiles, 2 * width, TILE), bf16),
        V((tiles, rows, TILE), f32),
        V((tiles, rows, TILE), f32),
        V((tiles, rows, TILE), bf16),
        V((tiles, rows, TILE), bf16),
        V((2 * half, LANES), f32),
        V((SN, 2 * half, LANES), f32),
        V((ITERS - 1, half, LANES), f32),
        V((ITERS - 1, SN, half, LANES), f32),
        V((half, LANES), f32),
        V((half, LANES), f32),
        V((rows, LANES), f32),
        V((rows, LANES), f32),
        V((rows, LANES), f32),
        V((rows, LANES), f32),
        V((ITERS, blocks, LANES), f32),
        V((ITERS, PN, blocks, LANES), f32),
        V((2 * blocks, LANES), f32),
        V((PN, 2 * blocks, LANES), f32),
        V((2, rows, 2 * width), f32),
        V((2, rows, width), f32),
        V((4, 2, chunk // 2, width), f32),
        V((4, 2, chunk, width), f32),
        V((4, ZN, piece, width), f32),
        V((4, ZN, piece, width), f32),
        V((2, ZN, piece, width), f32),
        V((rows, width), f32),
        V((tiles, width // 2, TILE), f32),
        V((tiles, 2, width // SN // 2, TILE), f32),
        V((tiles, 2, width // SN, TILE), f32),
        DMA((2 + tiles,)),
        DMA((ITERS,)),
        DMA((ITERS,)),
        DMA((ITERS,)),
        DMA((ITERS,)),
        DMA((2,)),
        DMA((4, 10)),
        DMA((4, 10)),
        DMA((6,)),
        DMA((6,)),
        DMA((tiles,)),
        DMA((tiles,)),
        DMA((tiles, 6)),
        DMA((tiles, 6)),
        pltpu.SemaphoreType.REGULAR,
        V((2, rows, TILE), bf16),
        V((2, rows, TILE), bf16),
        V((rows, TILE), f32),
        V((rows, TILE), f32),
    ]
    flops = 2 * rows * width * protos
    shapes = (
        jax.ShapeDtypeStruct((rows, width), f32),
        jax.ShapeDtypeStruct((width // SN, protos), f32),
    )
    outs = pl.pallas_call(
        functools.partial(kernel, SN, PN),
        out_shape=tuple(V(o.shape, o.dtype) for o in shapes),
        in_specs=[pl.BlockSpec(memory_space=pl.ANY)] * 3,
        out_specs=(pl.BlockSpec(memory_space=pltpu.VMEM),) * 2,
        scratch_shapes=scratch,
        compiler_params=pltpu.CompilerParams(
            collective_id=0, has_side_effects=True, vmem_limit_bytes=60 * 1024 * 1024
        ),
        cost_estimate=pl.CostEstimate(
            flops=12 * flops, bytes_accessed=4 * width * (protos + 4 * rows), transcendentals=2 * rows * protos
        ),
    )(teacher_feats, student_feats, prototypes)
    return pl.pallas_call(
        finish,
        out_shape=shapes,
        in_specs=[pl.BlockSpec(memory_space=pltpu.VMEM)] * 2,
        out_specs=(pl.BlockSpec(memory_space=pl.ANY),) * 2,
        scratch_shapes=[DMA((4,))],
        compiler_params=pltpu.CompilerParams(vmem_limit_bytes=4 * 1024 * 1024),
        cost_estimate=pl.CostEstimate(
            flops=0, bytes_accessed=8 * (rows * width + width // SN * protos), transcendentals=0
        ),
    )(*outs)


def solution(mesh):
    SN, PN = mesh.shape["smp"], mesh.shape["proto"]
    in_specs = (P("smp", None), P("smp", None), P(None, "proto"))
    out_specs = (P("smp", None), P("smp", "proto"))
    return jax.shard_map(
        functools.partial(local, SN, PN), mesh=mesh, in_specs=in_specs, out_specs=out_specs, check_vma=False
    )
```
